256 devices in a mesh: group: 32 (over z, x), head: 8 (over y, core).
Axes of the slice: x: 4, y: 4, z: 8, core: 2. Of those that a mesh axis runs over, the one named last changes fastest.
Arguments:
- noisy_qkv: bfloat16 [32768, 3, 3072], P(('group', 'head')), may hold values from -8 to 8
- clean_kv: bfloat16 [32768, 2, 3072], P('group', None, 'head'), may hold values from -8 to 8
- video_lengths: int32 [4], replicated, may hold values from 1 to 20, 32 in all
- pattern: int32 [4, 4], replicated, may hold values 0 or 1
Outputs:
- attended: bfloat16 [32768, 3072], P(('group', 'head'))
The draws below stay inside these ranges and needn't reach their ends.
Inputs may be any that keep to these rules, and one draw needn't show every extreme that they name: `video_lengths`: the largest entry is exactly 20.
All inputs are finite; a program needn't handle non-finite values.
Results may differ from the reference program's by a relative error of at most 0.0065.
Values may be sent and summed in bfloat16 or wider, within the bound.
A program may use at most 192 MiB of HBM per device.

```python
import math
import jax
import jax.numpy as jnp
import numpy as np
from jax import lax

HEADS = 24
HEAD_DIM = 128
CT = 1024
REACH = 4
GROUPS = 32
VIDEOS = 4
LONGEST = 20
TOKENS = 32768
N_GROUP = 32


def draw_noisy_qkv(key, part):
    key = jax.random.fold_in(key, 1)
    shape = (TOKENS, 3, HEADS * HEAD_DIM)
    base = jnp.clip(jax.random.normal(key, shape, jnp.float32), -6.0, 6.0)
    return base.astype(jnp.bfloat16)


def draw_clean_kv(key, part):
    key = jax.random.fold_in(key, 2)
    shape = (TOKENS, 2, HEADS * HEAD_DIM)
    base = jnp.clip(jax.random.normal(key, shape, jnp.float32), -6.0, 6.0)
    return base.astype(jnp.bfloat16)


def set_ends(values, key, low, high):
    longest = values.shape.index(max(values.shape))
    spots = []
    for shift in (0, 1):
        where = [jax.random.randint(jax.random.fold_in(key, axis), (), 0, length) for axis, length in enumerate(values.shape)]
        where[longest] = (where[longest] + shift) % values.shape[longest]
        spots.append(tuple(where))
    return values.at[spots[0]].set(low).at[spots[1]].set(high)


def split_up(number_of, total, bound, slope):
    weights = [(1 << 20) // math.isqrt(rank ** slope) + 1 for rank in range(2, number_of + 1)]
    surplus, counts = total - bound - (number_of - 1), [1] * (number_of - 1)
    while surplus > 0:
        candidates = [i for i in range(number_of - 1) if counts[i] < bound]
        pool, budget = sum([weights[i] for i in candidates]), surplus
        for i in candidates:
            more = min(bound - counts[i], max(1, budget * weights[i] // pool), surplus)
            counts[i] = counts[i] + more
            surplus = surplus - more
    return np.array([bound] + counts)


def ragged_sizes(rng, number_of, total, most, slope):
    if number_of == 2:
        one = jax.random.randint(rng, (), max(1, total - most), min(most, total - 1) + 1)
        return jnp.stack([one, total - one])
    sizes = jnp.asarray(split_up(number_of, total, most, slope), jnp.int32)
    pairs = (number_of - 1) // 2
    source_of, receiver = sizes[1:1 + 2 * pairs:2], sizes[2:2 + 2 * pairs:2]
    slack = jnp.minimum(source_of - 1, most - receiver)
    passed = jax.random.randint(jax.random.fold_in(rng, 1), (pairs,), 0, 1 << 20) % (slack + 1)
    sizes = sizes.at[1:1 + 2 * pairs:2].set(source_of - passed).at[2:2 + 2 * pairs:2].set(receiver + passed)
    return sizes[jax.random.permutation(jax.random.fold_in(rng, 2), number_of)]


def setup_inputs(seed: int = 0) -> dict:
    streams_of = jax.random.split(jax.random.key(seed), 5)
    noisy_qkv = draw_noisy_qkv(jax.random.fold_in(streams_of[4], 71), 0)
    clean_kv = draw_clean_kv(jax.random.fold_in(streams_of[4], 71), 0)
    video_lengths = ragged_sizes(streams_of[2], VIDEOS, GROUPS, LONGEST, 2).astype(jnp.int32)
    pattern = set_ends((jax.random.randint(streams_of[3], (VIDEOS, REACH), 0, 8) < 7).astype(jnp.int32), jax.random.fold_in(streams_of[3], 1), 0, 1)
    return dict(noisy_qkv=noisy_qkv, clean_kv=clean_kv, video_lengths=video_lengths, pattern=pattern)


def reference(noisy_qkv, clean_kv, video_lengths, pattern):
    ends = jnp.cumsum(video_lengths).astype(jnp.int32)
    noisy = noisy_qkv.reshape(N_GROUP, CT, 3, HEADS, HEAD_DIM)
    clean = clean_kv.reshape(N_GROUP, CT, 2, HEADS, HEAD_DIM)
    clean = jnp.concatenate([jnp.zeros((REACH, CT, 2, HEADS, HEAD_DIM), clean.dtype), clean], axis=0)
    scale = HEAD_DIM ** -0.5
    video_index = jnp.arange(VIDEOS, dtype=jnp.int32)

    def one_group(group_index):
        group_index = group_index.astype(jnp.int32)
        video = jnp.sum((ends <= group_index).astype(jnp.int32)).astype(jnp.int32)
        picked = video_index == video
        first = jnp.sum(jnp.where(picked, ends - video_lengths, 0)).astype(jnp.int32)
        row = jnp.sum(jnp.where(picked[:, None], pattern, 0), axis=0).astype(jnp.int32)
        own = lax.dynamic_index_in_dim(noisy, group_index, 0, keepdims=False)
        window = lax.dynamic_slice_in_dim(clean, group_index, REACH, 0)
        hops = REACH - jnp.arange(REACH, dtype=jnp.int32)
        valid = (group_index - hops >= first) & (row[hops - 1] == 1)
        keep = jnp.concatenate([jnp.ones((CT,), bool), jnp.repeat(valid, CT)])
        keys = jnp.concatenate([own[:, 1], window[:, :, 0].reshape(REACH * CT, HEADS, HEAD_DIM)], axis=0)
        values = jnp.concatenate([own[:, 2], window[:, :, 1].reshape(REACH * CT, HEADS, HEAD_DIM)], axis=0)
        queries = jnp.transpose(own[:, 0], (1, 0, 2)).astype(jnp.float32)
        keys = jnp.transpose(keys, (1, 0, 2)).astype(jnp.float32)
        values = jnp.transpose(values, (1, 0, 2)).astype(jnp.float32)

        def one_head(operands):
            query, key, value = operands
            scores = jnp.einsum("qd,kd->qk", query, key) * scale
            scores = jnp.where(keep[None, :], scores, -1e30)
            largest = jnp.max(scores, axis=1, keepdims=True)
            expo = jnp.where(keep[None, :], jnp.exp(scores - largest), 0.0)
            total = jnp.sum(expo, axis=1, keepdims=True)
            weights = lax.optimization_barrier(expo.astype(jnp.bfloat16)).astype(jnp.float32)
            return jnp.einsum("qk,kd->qd", weights, value) / total

        result = lax.map(one_head, (queries, keys, values))
        return jnp.transpose(result, (1, 0, 2)).astype(jnp.bfloat16).reshape(CT, HEADS * HEAD_DIM)

    out = lax.map(one_group, jnp.arange(N_GROUP, dtype=jnp.int32))
    return out.reshape(TOKENS, HEADS * HEAD_DIM)
```

```python
import functools

import jax
import jax.numpy as jnp
from jax import lax
from jax.experimental import pallas as pl
from jax.experimental.pallas import tpu as pltpu
from jax.sharding import PartitionSpec as P

MESH = pl.DeviceIdType.MESH
HEAD_DIM = 128
REACH = 4
ROW = 4
EXP2_SCALE = HEAD_DIM ** (-0.5) * 1.4426950408889634
FAR = 1e30

NOISY, OWN, ABOVE, ACROSS = 0, 1, 2, 3
MINE, PARTNER = 0, 1

STEPS = (
    (ABOVE, MINE, 0),
    (ACROSS, MINE, 0),
    (None, PARTNER, 0),
    (ACROSS, PARTNER, 0),
    (NOISY, MINE, 0),
    (ABOVE, MINE, 1),
    (NOISY, MINE, 1),
    (None, PARTNER, 1),
    (ACROSS, PARTNER, 1),
    (ACROSS, MINE, 1),
    (ABOVE, MINE, 2),
    (NOISY, MINE, 2),
    (None, PARTNER, 2),
    (ACROSS, PARTNER, 2),
    (ACROSS, MINE, 2),
)


def lookup(step, values):
    out = jnp.int32(values[0])
    for i, value in enumerate(values):
        if i and value != values[0]:
            out = jnp.where(step == i, jnp.int32(value), out)
    return out


def validity(group, lengths_ref, pattern_ref):
    videos = lengths_ref.shape[0]
    video, end = jnp.int32(0), jnp.int32(0)
    starts = []
    for j in range(videos):
        starts.append(end)
        end = end + lengths_ref[j]
        video = video + jnp.where(end <= group, 1, 0)
    first = jnp.int32(0)
    row = [jnp.int32(0)] * REACH
    for j in range(videos):
        first = jnp.where(video == j, starts[j], first)
        row = [jnp.where(video == j, pattern_ref[j, h], row[h]) for h in range(REACH)]
    return [(group - (h + 1) >= first) & (row[h] == 1) for h in range(REACH)]


def kernel(
    groups, heads_axis,
    noisy_ref, clean_ref, lengths_ref, pattern_ref, out_ref,
    query, keyval, accum, peak, total, part, part_stat, got, got_stat, final,
    noisy_send, noisy_recv, clean_send, clean_recv, query_send, query_recv,
    part_send, part_recv, out_send, out_recv, local_sem,
):
    group, head = lax.axis_index("group"), lax.axis_index("head")
    rows = noisy_ref.shape[1]
    width = keyval.shape[3]
    heads_here = width // HEAD_DIM
    column = lax.rem(group, ROW)
    odd = lax.rem(column, 2)
    near = group + 1 - 2 * odd
    far = group - column + (ROW - 1) - column
    below = lax.rem(group + ROW, groups)
    above = lax.rem(group + groups - ROW, groups)
    peers = [lax.rem(head + k, heads_axis) for k in range(1, heads_axis)]

    mine_ok = validity(group, lengths_ref, pattern_ref)
    near_ok = validity(near, lengths_ref, pattern_ref)

    def remote(src, dst, send, recv, to_group, to_head):
        return pltpu.make_async_remote_copy(
            src_ref=src, dst_ref=dst, send_sem=send, recv_sem=recv,
            device_id=(to_group, to_head), device_id_type=MESH,
        )

    def columns(index):
        return pl.ds(pl.multiple_of(index * width, width), width)

    def lanes(h):
        return pl.ds(h * HEAD_DIM, HEAD_DIM)

    my_rows = pl.ds(pl.multiple_of(head * rows, rows), rows)

    def noisy_target(which):
        return query.at[MINE] if which == 0 else keyval.at[NOISY, which - 1]

    def noisy_copy(which, k):
        to = peers[k]
        return remote(
            noisy_ref.at[which, :, columns(to)], noisy_target(which).at[my_rows, :],
            noisy_send.at[which, k], noisy_recv.at[which, k], group, to,
        )

    def noisy_local(which):
        return pltpu.make_async_copy(
            noisy_ref.at[which, :, columns(head)], noisy_target(which).at[my_rows, :], local_sem.at[which]
        )

    def own_copy(which):
        return pltpu.make_async_copy(clean_ref.at[which], keyval.at[OWN, which], local_sem.at[3 + which])

    def above_copy(h, which):
        return remote(
            clean_ref.at[which, :, lanes(h)], keyval.at[ABOVE, which, :, lanes(h)],
            clean_send.at[0, h, which], clean_recv.at[0, h, which], below, head,
        )

    def across_copy(h, which, relay):
        src = keyval.at[ABOVE] if relay else clean_ref
        return remote(
            src.at[which, :, lanes(h)], keyval.at[ACROSS, which, :, lanes(h)],
            clean_send.at[1, h, which], clean_recv.at[1, h, which], far, head,
        )

    def query_copy(h):
        return remote(
            query.at[MINE, :, lanes(h)], query.at[PARTNER, :, lanes(h)],
            query_send.at[h], query_recv.at[h], near, head,
        )

    def part_copy(h):
        return remote(part.at[h], got.at[h], part_send.at[h, 0], part_recv.at[h, 0], near, head)

    def stat_copy(h):
        return remote(part_stat.at[h], got_stat.at[h], part_send.at[h, 1], part_recv.at[h, 1], near, head)

    def out_columns(h):
        return pl.ds(pl.multiple_of((head * heads_here + h) * HEAD_DIM, HEAD_DIM), HEAD_DIM)

    def out_copy(h, k):
        to = peers[k]
        return remote(
            final.at[h, pl.ds(pl.multiple_of(to * rows, rows), rows), :], out_ref.at[:, out_columns(h)],
            out_send.at[h, k], out_recv.at[h, k], group, to,
        )

    def out_local(h):
        return pltpu.make_async_copy(final.at[h, my_rows, :], out_ref.at[:, out_columns(h)], local_sem.at[5 + h])

    barrier = pltpu.get_barrier_semaphore()
    for to in peers:
        pl.semaphore_signal(barrier, inc=1, device_id=(group, to), device_id_type=MESH)
    for to in (near, far, below, above):
        pl.semaphore_signal(barrier, inc=1, device_id=(to, head), device_id_type=MESH)
    pl.semaphore_wait(barrier, len(peers) + 4)

    others = range(len(peers))
    both = range(2)
    for k in others:
        noisy_copy(0, k).start()
    noisy_local(0).start()
    for h in range(heads_here):
        for which in both:
            above_copy(h, which).start()

            @pl.when(column < 2)
            def _():
                across_copy(h, which, False).start()

    for which in (1, 2):
        noisy_local(which).start()
        own_copy(which - 1).start()
    accum[...] = jnp.zeros_like(accum)
    total[...] = jnp.zeros_like(total)
    peak[...] = jnp.full_like(peak, -FAR)

    noisy_local(0).wait()
    for k in others:
        noisy_copy(0, k).wait_recv()
    for h in range(heads_here):
        query_copy(h).start()
    for which in (1, 2):
        for k in others:
            noisy_copy(which, k).start()

    def attend(slot, whose, h, keep):
        lane = pl.ds(pl.multiple_of(h * HEAD_DIM, HEAD_DIM), HEAD_DIM)
        scores = lax.dot_general(
            keyval[slot, 0, :, lane], query[whose, :, lane], (((1,), (1,)), ((), ())),
            preferred_element_type=jnp.float32,
        )
        before = peak[whose, h]
        largest = jnp.where(keep, jnp.max(scores, axis=0, keepdims=True), -FAR)
        now = jnp.maximum(before, largest)
        expo = jnp.exp2((scores - jnp.where(keep, now, FAR)) * EXP2_SCALE)
        factor = jnp.exp2((before - now) * EXP2_SCALE)
        added = lax.dot_general(
            keyval[slot, 1, :, lane], expo.astype(jnp.bfloat16), (((0,), (0,)), ((), ())),
            preferred_element_type=jnp.float32,
        )
        peak[whose, h] = now
        total[whose, h] = total[whose, h] * factor + jnp.sum(expo, axis=0, keepdims=True)
        accum[whose, h] = accum[whose, h] * factor + added

    def merge(h):
        part_copy(h).wait_recv()
        stat_copy(h).wait_recv()
        here, there = peak[MINE, h], got_stat[h, 0:1, :]
        now = jnp.maximum(here, there)
        a = jnp.exp2((here - now) * EXP2_SCALE)
        b = jnp.exp2((there - now) * EXP2_SCALE)
        inverse = 1.0 / (total[MINE, h] * a + got_stat[h, 1:2, :] * b)
        summed = accum[MINE, h] * (a * inverse) + got[h].astype(jnp.float32) * (b * inverse)
        final[h] = jnp.transpose(summed).astype(final.dtype)
        for k in others:
            out_copy(h, k).start()
        out_local(h).start()

    def hand_over(h):
        part[h] = accum[PARTNER, h].astype(part.dtype)
        part_stat[h, 0:1, :] = peak[PARTNER, h]
        part_stat[h, 1:2, :] = total[PARTNER, h]
        part_copy(h).start()
        stat_copy(h).start()

    def take_above(h):
        for which in both:
            above_copy(h, which).wait_recv()

            @pl.when(column >= 2)
            def _():
                across_copy(h, which, True).start()

    def take_across(h):
        for which in both:
            across_copy(h, which, False).wait_recv()

    def take_noisy():
        for which in (1, 2):
            noisy_local(which).wait()
            for k in others:
                noisy_copy(which, k).wait_recv()

    def take_own():
        for which in both:
            own_copy(which).wait()

    hooks = {}
    seen = set()
    for i, (slot, whose, h) in enumerate(STEPS):
        todo = hooks.setdefault(i, [])
        if whose == PARTNER and ("query", h) not in seen:
            seen.add(("query", h))
            todo.append(functools.partial(lambda h: query_copy(h).wait_recv(), h))
        if slot is None and "own" not in seen:
            seen.add("own")
            todo.append(take_own)
        if slot == ABOVE:
            todo.append(functools.partial(take_above, h))
        if slot == ACROSS and ("across", h) not in seen:
            seen.add(("across", h))
            todo.append(functools.partial(take_across, h))
        if slot == NOISY and "noisy" not in seen:
            seen.add("noisy")
            todo.append(take_noisy)
    after = {}
    for h in range(heads_here):
        last = max(i for i, (_, whose, of) in enumerate(STEPS) if whose == PARTNER and of == h)
        after.setdefault(last, []).append(functools.partial(hand_over, h))
    merge_after = {10: 0, 13: 1, 14: 2}
    for i, h in merge_after.items():
        after.setdefault(i, []).append(functools.partial(merge, h))

    def distance(slot, whose, is_odd):
        if slot == NOISY:
            return -1
        if whose == MINE:
            return 3 if slot == ABOVE else (2 if is_odd else 0)
        return 1 if slot == ACROSS else (2 if is_odd else 0)

    def one(step, carry):
        for i, todo in hooks.items():
            if todo:

                @pl.when(step == i)
                def _():
                    for act in todo:
                        act()

        shared = jnp.where(odd == 1, ABOVE, OWN)
        slot = lookup(step, [-1 if s is None else s for s, _, _ in STEPS])
        slot = jnp.where(slot < 0, shared, slot)
        whose = lookup(step, [w for _, w, _ in STEPS])
        h = lookup(step, [h for _, _, h in STEPS])
        at = jnp.where(
            odd == 1,
            lookup(step, [distance(s, w, True) for s, w, _ in STEPS]),
            lookup(step, [distance(s, w, False) for s, w, _ in STEPS]),
        )
        keep = at < 0
        for j in range(REACH):
            keep = keep | ((at == j) & jnp.where(whose == MINE, mine_ok[j], near_ok[j]))
        attend(slot, whose, h, keep)
        for i, todo in after.items():

            @pl.when(step == i)
            def _():
                for act in todo:
                    act()

        return carry

    lax.fori_loop(0, len(STEPS), one, 0)

    for h in range(heads_here):
        out_local(h).wait()
        query_copy(h).wait_send()
        part_copy(h).wait_send()
        stat_copy(h).wait_send()
        for which in both:
            above_copy(h, which).wait_send()
            across_copy(h, which, False).wait_send()
        for k in others:
            out_copy(h, k).wait()
            noisy_copy(h, k).wait_send()


def on_device(groups, heads_axis, noisy_qkv, clean_kv, video_lengths, pattern):
    noisy = jnp.transpose(noisy_qkv, (1, 0, 2))
    clean = jnp.transpose(clean_kv, (1, 0, 2))
    _, tokens, width = clean.shape
    heads_here = width // HEAD_DIM
    rows, features = noisy.shape[1:]
    dma = pltpu.SemaphoreType.DMA
    peers = heads_axis - 1
    flops = 2 * 2 * tokens * tokens * width * (REACH + 1)
    return pl.pallas_call(
        functools.partial(kernel, groups, heads_axis),
        out_shape=jax.ShapeDtypeStruct((rows, features), noisy.dtype),
        in_specs=[pl.BlockSpec(memory_space=pl.ANY)] * 2 + [pl.BlockSpec(memory_space=pltpu.SMEM)] * 2,
        out_specs=pl.BlockSpec(memory_space=pl.ANY),
        scratch_shapes=[
            pltpu.VMEM((2, tokens, width), noisy.dtype),
            pltpu.VMEM((4, 2, tokens, width), noisy.dtype),
            pltpu.VMEM((2, heads_here, HEAD_DIM, tokens), jnp.float32),
            pltpu.VMEM((2, heads_here, 1, tokens), jnp.float32),
            pltpu.VMEM((2, heads_here, 1, tokens), jnp.float32),
            pltpu.VMEM((heads_here, HEAD_DIM, tokens), noisy.dtype),
            pltpu.VMEM((heads_here, 2, tokens), jnp.float32),
            pltpu.VMEM((heads_here, HEAD_DIM, tokens), noisy.dtype),
            pltpu.VMEM((heads_here, 2, tokens), jnp.float32),
            pltpu.VMEM((heads_here, tokens, HEAD_DIM), noisy.dtype),
            dma((3, peers)), dma((3, peers)),
            dma((2, heads_here, 2)), dma((2, heads_here, 2)),
            dma((heads_here,)), dma((heads_here,)),
            dma((heads_here, 2)), dma((heads_here, 2)),
            dma((heads_here, peers)), dma((heads_here, peers)),
            dma((5 + heads_here,)),
        ],
        compiler_params=pltpu.CompilerParams(
            collective_id=0, has_side_effects=True, vmem_limit_bytes=56 * 2**20
        ),
        cost_estimate=pl.CostEstimate(
            flops=flops, bytes_accessed=8 * tokens * width, transcendentals=tokens * tokens * heads_here * (REACH + 1)
        ),
    )(noisy, clean, video_lengths, pattern)


def solution(mesh):
    groups, heads_axis = mesh.shape["group"], mesh.shape["head"]
    return jax.shard_map(
        functools.partial(on_device, groups, heads_axis),
        mesh=mesh,
        in_specs=(P(("group", "head"), None, None), P("group", None, "head"), P(), P()),
        out_specs=P(("group", "head"), None),
        check_vma=False,
    )
```

```python
import functools

import jax
import jax.numpy as jnp
from jax import lax
from jax.experimental import pallas as pl
from jax.experimental.pallas import tpu as pltpu
from jax.sharding import PartitionSpec as P

MESH = pl.DeviceIdType.MESH
HEAD_DIM = 128
REACH = 4
ROW = 4
EXP2_SCALE = HEAD_DIM ** (-0.5) * 1.4426950408889634
FAR = 1e30

NOISY, OWN, ABOVE, ACROSS = 0, 1, 2, 3
MINE, PARTNER = 0, 1

SPLIT = 2
TILES = 2

STEPS = (
    (ABOVE, MINE, 0),
    (ACROSS, MINE, 0),
    (None, PARTNER, 0),
    (ACROSS, PARTNER, 0),
    (ABOVE, MINE, 1),
    (None, PARTNER, 1),
    (NOISY, MINE, 0),
    (ACROSS, PARTNER, 1),
    (ACROSS, MINE, 1),
    (NOISY, MINE, 1),
    (NOISY, MINE, 2),
    (ABOVE, MINE, 2),
    (None, PARTNER, 2),
)
PASS_ON = {0: (2, 3), 1: (4,), 3: (5,), 4: (6, 7), 6: (8,), 8: (9,), 9: (10,), 11: (11,)}
HAND_OVER_AFTER = {3: 0, 7: 1}
MERGE_AFTER = {10: 0}


def lookup(step, values):
    out = jnp.int32(values[0])
    for i, value in enumerate(values):
        if i and value != values[0]:
            out = jnp.where(step == i, jnp.int32(value), out)
    return out


def validity(group, lengths_ref, pattern_ref):
    videos = lengths_ref.shape[0]
    video, end = jnp.int32(0), jnp.int32(0)
    starts = []
    for j in range(videos):
        starts.append(end)
        end = end + lengths_ref[j]
        video = video + jnp.where(end <= group, 1, 0)
    first = jnp.int32(0)
    row = [jnp.int32(0)] * REACH
    for j in range(videos):
        first = jnp.where(video == j, starts[j], first)
        row = [jnp.where(video == j, pattern_ref[j, h], row[h]) for h in range(REACH)]
    return [(group - (h + 1) >= first) & (row[h] == 1) for h in range(REACH)]


def kernel(
    groups, heads_axis,
    noisy_ref, clean_ref, lengths_ref, pattern_ref, out_ref,
    query, keyval, accum, peak, total, part, part_stat, got, got_stat, final,
    noisy_send, noisy_recv, clean_send, clean_recv, query_send, query_recv,
    part_send, part_recv, out_send, out_recv, local_sem,
):
    group, head = lax.axis_index("group"), lax.axis_index("head")
    rows = noisy_ref.shape[1]
    width = keyval.shape[3]
    heads_here = width // HEAD_DIM
    column = lax.rem(group, ROW)
    odd = lax.rem(column, 2)
    near = group + 1 - 2 * odd
    far = group - column + (ROW - 1) - column
    below = lax.rem(group + ROW, groups)
    above = lax.rem(group + groups - ROW, groups)
    peers = [lax.rem(head + k, heads_axis) for k in range(1, heads_axis)]

    mine_ok = validity(group, lengths_ref, pattern_ref)
    near_ok = validity(near, lengths_ref, pattern_ref)

    def remote(src, dst, send, recv, to_group, to_head):
        return pltpu.make_async_remote_copy(
            src_ref=src, dst_ref=dst, send_sem=send, recv_sem=recv,
            device_id=(to_group, to_head), device_id_type=MESH,
        )

    def columns(index):
        return pl.ds(pl.multiple_of(index * width, width), width)

    def lanes(h):
        return pl.ds(h * HEAD_DIM, HEAD_DIM)

    my_rows = pl.ds(pl.multiple_of(head * rows, rows), rows)

    def noisy_target(which):
        return query.at[MINE] if which == 0 else keyval.at[NOISY, which - 1]

    def noisy_copy(which, k):
        to = peers[k]
        return remote(
            noisy_ref.at[which, :, columns(to)], noisy_target(which).at[my_rows, :],
            noisy_send.at[which, k], noisy_recv.at[which, k], group, to,
        )

    def noisy_local(which):
        return pltpu.make_async_copy(
            noisy_ref.at[which, :, columns(head)], noisy_target(which).at[my_rows, :], local_sem.at[which]
        )

    def own_copy(which):
        return pltpu.make_async_copy(clean_ref.at[which], keyval.at[OWN, which], local_sem.at[3 + which])

    def piece(i):
        h, rest = divmod(i, 2 * SPLIT)
        which, part_of = divmod(rest, SPLIT)
        n = keyval.shape[2] // SPLIT
        return which, pl.ds(part_of * n, n), lanes(h)

    pieces = range(heads_here * 2 * SPLIT)

    def above_copy(i):
        at = piece(i)
        return remote(
            clean_ref.at[at], keyval.at[(ABOVE, *at)], clean_send.at[0, i], clean_recv.at[0, i], below, head
        )

    def across_copy(i, relay):
        at = piece(i)
        src = keyval.at[(ABOVE, *at)] if relay else clean_ref.at[at]
        return remote(src, keyval.at[(ACROSS, *at)], clean_send.at[1, i], clean_recv.at[1, i], far, head)

    def query_copy(h):
        return remote(
            query.at[MINE, :, lanes(h)], query.at[PARTNER, :, lanes(h)],
            query_send.at[h], query_recv.at[h], near, head,
        )

    tokens = query.shape[1]

    def part_copies(h, tile=None):
        at = pl.ds(0, tokens) if tile is None else pl.ds(tile * (tokens // TILES), tokens // TILES)
        sem = h if tile is None else h + tile
        return (
            remote(part.at[h, :, at], got.at[h, :, at], part_send.at[sem, 0], part_recv.at[sem, 0], near, head),
            remote(
                part_stat.at[h, :, at], got_stat.at[h, :, at], part_send.at[sem, 1], part_recv.at[sem, 1], near, head
            ),
        )

    def out_columns(h):
        return pl.ds(pl.multiple_of((head * heads_here + h) * HEAD_DIM, HEAD_DIM), HEAD_DIM)

    def out_copy(h, to):
        k = lax.rem(to - head + heads_axis, heads_axis)
        return remote(
            final.at[h, pl.ds(pl.multiple_of(to * rows, rows), rows), :], out_ref.at[:, out_columns(h)],
            out_send.at[h, k], out_recv.at[h, k], group, to,
        )

    def out_local(h):
        return pltpu.make_async_copy(final.at[h, my_rows, :], out_ref.at[:, out_columns(h)], local_sem.at[5 + h])

    barrier = pltpu.get_barrier_semaphore()
    for to in peers:
        pl.semaphore_signal(barrier, inc=1, device_id=(group, to), device_id_type=MESH)
    for to in (near, far, below, above):
        pl.semaphore_signal(barrier, inc=1, device_id=(to, head), device_id_type=MESH)
    pl.semaphore_wait(barrier, len(peers) + 4)

    others = range(len(peers))
    for k in others:
        noisy_copy(0, k).start()
    noisy_local(0).start()
    for i in pieces:
        above_copy(i).start()

    @pl.when(column < 2)
    def _():
        for i in pieces:
            across_copy(i, False).start()

    for which in (1, 2):
        noisy_local(which).start()
        own_copy(which - 1).start()
    accum[...] = jnp.zeros_like(accum)
    total[...] = jnp.zeros_like(total)
    peak[...] = jnp.full_like(peak, -FAR)

    def pass_on(i):
        above_copy(i).wait_recv()

        @pl.when(column >= 2)
        def _():
            across_copy(i, True).start()

    for i in range(PASS_ON[0][0]):
        pass_on(i)
    noisy_local(0).wait()
    for k in others:
        noisy_copy(0, k).wait_recv()
    for h in range(heads_here):
        query_copy(h).start()
    for which in (1, 2):
        for k in others:
            noisy_copy(which, k).start()

    def attend(slot, whose, h, keep, at):
        lane = pl.ds(pl.multiple_of(h * HEAD_DIM, HEAD_DIM), HEAD_DIM)
        scores = lax.dot_general(
            keyval[slot, 0, :, lane], query[whose, at, lane], (((1,), (1,)), ((), ())),
            preferred_element_type=jnp.float32,
        )
        before = peak[whose, h, :, at]
        largest = jnp.where(keep, jnp.max(scores, axis=0, keepdims=True), -FAR)
        now = jnp.maximum(before, largest)
        expo = jnp.exp2((scores - jnp.where(keep, now, FAR)) * EXP2_SCALE)
        factor = jnp.exp2((before - now) * EXP2_SCALE)
        added = lax.dot_general(
            keyval[slot, 1, :, lane], expo.astype(jnp.bfloat16), (((0,), (0,)), ((), ())),
            preferred_element_type=jnp.float32,
        )
        peak[whose, h, :, at] = now
        total[whose, h, :, at] = total[whose, h, :, at] * factor + jnp.sum(expo, axis=0, keepdims=True)
        accum[whose, h, :, at] = accum[whose, h, :, at] * factor + added

    every = pl.ds(0, tokens)

    def tile_of(t):
        return pl.ds(t * (tokens // TILES), tokens // TILES)

    def merge(h, tile=None):
        at = every if tile is None else tile_of(tile)
        for copy in part_copies(h, tile):
            copy.wait_recv()
        here, there = peak[MINE, h, :, at], got_stat[h, 0:1, at]
        now = jnp.maximum(here, there)
        a = jnp.exp2((here - now) * EXP2_SCALE)
        b = jnp.exp2((there - now) * EXP2_SCALE)
        inverse = 1.0 / (total[MINE, h, :, at] * a + got_stat[h, 1:2, at] * b)
        summed = accum[MINE, h, :, at] * (a * inverse) + got[h, :, at].astype(jnp.float32) * (b * inverse)
        final[h, at, :] = jnp.transpose(summed).astype(final.dtype)
        for j in range(at.start // rows, (at.start + at.size) // rows):

            @pl.when(head != j)
            def _():
                out_copy(h, j).start()

            @pl.when(head == j)
            def _():
                out_local(h).start()

    def hand_over(h, tile=None):
        at = every if tile is None else tile_of(tile)
        part[h, :, at] = accum[PARTNER, h, :, at].astype(part.dtype)
        part_stat[h, 0:1, at] = peak[PARTNER, h, :, at]
        part_stat[h, 1:2, at] = total[PARTNER, h, :, at]
        for copy in part_copies(h, tile):
            copy.start()

    def take_across(h):
        for i in pieces:
            if i // (2 * SPLIT) == h:
                across_copy(i, False).wait_recv()

    def take_noisy():
        for which in (1, 2):
            noisy_local(which).wait()
            for k in others:
                noisy_copy(which, k).wait_recv()

    def take_own():
        for which in range(2):
            own_copy(which).wait()

    hooks = {}
    seen = set()
    for i, (slot, whose, h) in enumerate(STEPS):
        todo = hooks.setdefault(i, [])
        for j in PASS_ON.get(i, ()):
            todo.append(functools.partial(pass_on, j))
        if whose == PARTNER and ("query", h) not in seen:
            seen.add(("query", h))
            todo.append(functools.partial(lambda h: query_copy(h).wait_recv(), h))
        if slot is None and "own" not in seen:
            seen.add("own")
            todo.append(take_own)
        if slot == ACROSS and ("across", h) not in seen:
            seen.add(("across", h))
            todo.append(functools.partial(take_across, h))
        if slot == NOISY and "noisy" not in seen:
            seen.add("noisy")
            todo.append(take_noisy)
    after = {}
    for i, h in HAND_OVER_AFTER.items():
        after.setdefault(i, []).append(functools.partial(hand_over, h))
    for i, h in MERGE_AFTER.items():
        after.setdefault(i, []).append(functools.partial(merge, h))

    def distance(slot, whose, is_odd):
        if slot == NOISY:
            return -1
        if whose == MINE:
            return 3 if slot == ABOVE else (2 if is_odd else 0)
        return 1 if slot == ACROSS else (2 if is_odd else 0)

    def one(step, carry):
        for i, todo in hooks.items():
            if todo:

                @pl.when(step == i)
                def _():
                    for act in todo:
                        act()

        shared = jnp.where(odd == 1, ABOVE, OWN)
        slot = lookup(step, [-1 if s is None else s for s, _, _ in STEPS])
        slot = jnp.where(slot < 0, shared, slot)
        whose = lookup(step, [w for _, w, _ in STEPS])
        h = lookup(step, [h for _, _, h in STEPS])
        at = jnp.where(
            odd == 1,
            lookup(step, [distance(s, w, True) for s, w, _ in STEPS]),
            lookup(step, [distance(s, w, False) for s, w, _ in STEPS]),
        )
        keep = at < 0
        for j in range(REACH):
            keep = keep | ((at == j) & jnp.where(whose == MINE, mine_ok[j], near_ok[j]))
        attend(slot, whose, h, keep, every)
        for i, todo in after.items():

            @pl.when(step == i)
            def _():
                for act in todo:
                    act()

        return carry

    lax.fori_loop(0, len(STEPS), one, 0)

    last = heads_here - 1
    take_across(last)
    for tile in range(TILES):
        attend(ACROSS, PARTNER, last, near_ok[1], tile_of(tile))
        hand_over(last, tile)
    merge(1)
    attend(ACROSS, MINE, last, (mine_ok[0] & (odd == 0)) | (mine_ok[2] & (odd == 1)), every)
    for tile in range(TILES):
        merge(last, tile)

    for h in range(heads_here):
        out_local(h).wait()
        query_copy(h).wait_send()
        for copy in [c for t in range(TILES) for c in part_copies(h, t)] if h == last else part_copies(h):
            copy.wait_send()
        for k in others:
            out_copy(h, peers[k]).wait()
            noisy_copy(h, k).wait_send()
    for i in pieces:
        above_copy(i).wait_send()
        across_copy(i, False).wait_send()


def on_device(groups, heads_axis, noisy_qkv, clean_kv, video_lengths, pattern):
    noisy = jnp.transpose(noisy_qkv, (1, 0, 2))
    clean = jnp.transpose(clean_kv, (1, 0, 2))
    _, tokens, width = clean.shape
    heads_here = width // HEAD_DIM
    rows, features = noisy.shape[1:]
    dma = pltpu.SemaphoreType.DMA
    peers = heads_axis - 1
    flops = 2 * 2 * tokens * tokens * width * (REACH + 1)
    return pl.pallas_call(
        functools.partial(kernel, groups, heads_axis),
        out_shape=jax.ShapeDtypeStruct((rows, features), noisy.dtype),
        in_specs=[pl.BlockSpec(memory_space=pl.ANY)] * 2 + [pl.BlockSpec(memory_space=pltpu.SMEM)] * 2,
        out_specs=pl.BlockSpec(memory_space=pl.ANY),
        scratch_shapes=[
            pltpu.VMEM((2, tokens, width), noisy.dtype),
            pltpu.VMEM((4, 2, tokens, width), noisy.dtype),
            pltpu.VMEM((2, heads_here, HEAD_DIM, tokens), jnp.float32),
            pltpu.VMEM((2, heads_here, 1, tokens), jnp.float32),
            pltpu.VMEM((2, heads_here, 1, tokens), jnp.float32),
            pltpu.VMEM((heads_here, HEAD_DIM, tokens), noisy.dtype),
            pltpu.VMEM((heads_here, 2, tokens), jnp.float32),
            pltpu.VMEM((heads_here, HEAD_DIM, tokens), noisy.dtype),
            pltpu.VMEM((heads_here, 2, tokens), jnp.float32),
            pltpu.VMEM((heads_here, tokens, HEAD_DIM), noisy.dtype),
            dma((3, peers)), dma((3, peers)),
            dma((2, heads_here * 2 * SPLIT)), dma((2, heads_here * 2 * SPLIT)),
            dma((heads_here,)), dma((heads_here,)),
            dma((heads_here - 1 + TILES, 2)), dma((heads_here - 1 + TILES, 2)),
            dma((heads_here, heads_axis)), dma((heads_here, heads_axis)),
            dma((5 + heads_here,)),
        ],
        compiler_params=pltpu.CompilerParams(
            collective_id=0, has_side_effects=True, vmem_limit_bytes=56 * 2**20
        ),
        cost_estimate=pl.CostEstimate(
            flops=flops, bytes_accessed=8 * tokens * width, transcendentals=tokens * tokens * heads_here * (REACH + 1)
        ),
    )(noisy, clean, video_lengths, pattern)


def solution(mesh):
    groups, heads_axis = mesh.shape["group"], mesh.shape["head"]
    return jax.shard_map(
        functools.partial(on_device, groups, heads_axis),
        mesh=mesh,
        in_specs=(P(("group", "head"), None, None), P("group", None, "head"), P(), P()),
        out_specs=P(("group", "head"), None),
        check_vma=False,
    )
```

```python
import functools

import jax
import jax.numpy as jnp
from jax import lax
from jax.experimental import pallas as pl
from jax.experimental.pallas import tpu as pltpu
from jax.sharding import PartitionSpec as P

MESH = pl.DeviceIdType.MESH
HEAD_DIM = 128
REACH = 4
ROW = 4
EXP2_SCALE = HEAD_DIM ** (-0.5) * 1.4426950408889634
FAR = 1e30

NOISY, OWN, ABOVE, ACROSS = 0, 1, 2, 3
MINE, PARTNER = 0, 1

SPLIT = 2
TILES = 2

STEPS = (
    (ABOVE, MINE, 0),
    (ACROSS, MINE, 0),
    (None, PARTNER, 0),
    (ACROSS, PARTNER, 0),
    (ABOVE, MINE, 1),
    (None, PARTNER, 1),
    (NOISY, MINE, 0),
    (ACROSS, PARTNER, 1),
    (ACROSS, MINE, 1),
    (NOISY, MINE, 1),
    (NOISY, MINE, 2),
    (ABOVE, MINE, 2),
    (None, PARTNER, 2),
)
PASS_ON = {0: (2, 3), 1: (4,), 3: (5,), 4: (6, 7), 6: (8,), 8: (9,), 9: (10,), 11: (11,)}
HAND_OVER_AFTER = {3: 0, 7: 1}
MERGE_AFTER = {10: 0}


def lookup(step, values):
    out = jnp.int32(values[0])
    for i, value in enumerate(values):
        if i and value != values[0]:
            out = jnp.where(step == i, jnp.int32(value), out)
    return out


def validity(group, lengths_ref, pattern_ref):
    videos = lengths_ref.shape[0]
    video, end = jnp.int32(0), jnp.int32(0)
    starts = []
    for j in range(videos):
        starts.append(end)
        end = end + lengths_ref[j]
        video = video + jnp.where(end <= group, 1, 0)
    first = jnp.int32(0)
    row = [jnp.int32(0)] * REACH
    for j in range(videos):
        first = jnp.where(video == j, starts[j], first)
        row = [jnp.where(video == j, pattern_ref[j, h], row[h]) for h in range(REACH)]
    return [(group - (h + 1) >= first) & (row[h] == 1) for h in range(REACH)]


def kernel(
    groups, heads_axis,
    noisy_ref, clean_ref, lengths_ref, pattern_ref, out_ref,
    paired, query, keyval, accum, peak, total, part, part_stat, got, got_stat, final,
    noisy_send, noisy_recv, clean_send, clean_recv, query_send, query_recv,
    part_send, part_recv, out_send, out_recv, local_sem,
):
    group, head = lax.axis_index("group"), lax.axis_index("head")
    rows = noisy_ref.shape[1]
    tokens, width = query.shape[1:]
    heads_here = width // HEAD_DIM
    column = lax.rem(group, ROW)
    odd = lax.rem(column, 2)
    near = group + 1 - 2 * odd
    far = group - column + (ROW - 1) - column
    below = lax.rem(group + ROW, groups)
    above = lax.rem(group + groups - ROW, groups)
    peers = [lax.rem(head + k, heads_axis) for k in range(1, heads_axis)]

    mine_ok = validity(group, lengths_ref, pattern_ref)
    near_ok = validity(near, lengths_ref, pattern_ref)

    def remote(src, dst, send, recv, to_group, to_head):
        return pltpu.make_async_remote_copy(
            src_ref=src, dst_ref=dst, send_sem=send, recv_sem=recv,
            device_id=(to_group, to_head), device_id_type=MESH,
        )

    def columns(index):
        return pl.ds(pl.multiple_of(index * width, width), width)

    def lanes(h):
        return pl.ds(h * HEAD_DIM, HEAD_DIM)

    my_rows = pl.ds(pl.multiple_of(head * rows, rows), rows)

    def noisy_target(which):
        return query.at[MINE] if which == 0 else keyval.at[NOISY, which - 1]

    def noisy_copy(which, k):
        to = peers[k]
        return remote(
            noisy_ref.at[which, :, columns(to)], noisy_target(which).at[my_rows, :],
            noisy_send.at[which, k], noisy_recv.at[which, k], group, to,
        )

    def noisy_local(which):
        return pltpu.make_async_copy(
            noisy_ref.at[which, :, columns(head)], noisy_target(which).at[my_rows, :], local_sem.at[which]
        )

    def paired_copy(h):
        return pltpu.make_async_copy(clean_ref.at[:, h], paired.at[h], local_sem.at[3 + h])

    def part_pairs(h):
        n = 2 * HEAD_DIM
        rows_of = paired.at[h].reshape(2 * tokens, HEAD_DIM)
        to, source = (lax.broadcasted_iota(jnp.int32, (n, n), axis) for axis in (0, 1))
        pick = source == 2 * lax.rem(to, HEAD_DIM) + to // HEAD_DIM
        pick = jnp.where(pick, 1.0, 0.0).astype(keyval.dtype)
        for i in range(2 * tokens // n):
            moved = jnp.dot(pick, rows_of[pl.ds(i * n, n), :], preferred_element_type=jnp.float32)
            moved = moved.astype(keyval.dtype)
            for which in range(2):
                keyval[OWN, which, pl.ds(i * HEAD_DIM, HEAD_DIM), lanes(h)] = moved[which * HEAD_DIM:(which + 1) * HEAD_DIM]

    def piece(i):
        h, rest = divmod(i, 2 * SPLIT)
        which, part_of = divmod(rest, SPLIT)
        n = keyval.shape[2] // SPLIT
        return which, pl.ds(part_of * n, n), lanes(h)

    pieces = range(heads_here * 2 * SPLIT)

    def above_copy(i):
        at = piece(i)
        return remote(
            keyval.at[(OWN, *at)], keyval.at[(ABOVE, *at)], clean_send.at[0, i], clean_recv.at[0, i], below, head
        )

    def across_copy(i, relay):
        at = piece(i)
        src = keyval.at[(ABOVE if relay else OWN, *at)]
        return remote(src, keyval.at[(ACROSS, *at)], clean_send.at[1, i], clean_recv.at[1, i], far, head)

    def query_copy(h):
        return remote(
            query.at[MINE, :, lanes(h)], query.at[PARTNER, :, lanes(h)],
            query_send.at[h], query_recv.at[h], near, head,
        )

    def part_copies(h, tile=None):
        at = pl.ds(0, tokens) if tile is None else pl.ds(tile * (tokens // TILES), tokens // TILES)
        sem = h if tile is None else h + tile
        return (
            remote(part.at[h, :, at], got.at[h, :, at], part_send.at[sem, 0], part_recv.at[sem, 0], near, head),
            remote(
                part_stat.at[h, :, at], got_stat.at[h, :, at], part_send.at[sem, 1], part_recv.at[sem, 1], near, head
            ),
        )

    def out_columns(h):
        return pl.ds(pl.multiple_of((head * heads_here + h) * HEAD_DIM, HEAD_DIM), HEAD_DIM)

    def out_copy(h, to):
        k = lax.rem(to - head + heads_axis, heads_axis)
        return remote(
            final.at[h, pl.ds(pl.multiple_of(to * rows, rows), rows), :], out_ref.at[:, out_columns(h)],
            out_send.at[h, k], out_recv.at[h, k], group, to,
        )

    def out_local(h):
        return pltpu.make_async_copy(final.at[h, my_rows, :], out_ref.at[:, out_columns(h)], local_sem.at[3 + heads_here + h])

    barrier = pltpu.get_barrier_semaphore()
    for to in peers:
        pl.semaphore_signal(barrier, inc=1, device_id=(group, to), device_id_type=MESH)
    for to in (near, far, below, above):
        pl.semaphore_signal(barrier, inc=1, device_id=(to, head), device_id_type=MESH)
    for h in range(heads_here):
        paired_copy(h).start()
    for which in range(3):
        noisy_local(which).start()
    others = range(len(peers))
    for h in range(heads_here):
        paired_copy(h).wait()
        part_pairs(h)
        if h == 0:
            pl.semaphore_wait(barrier, len(peers) + 4)
            for k in others:
                noisy_copy(0, k).start()
        for i in pieces:
            if i // (2 * SPLIT) == h:
                above_copy(i).start()

                @pl.when(column < 2)
                def _():
                    across_copy(i, False).start()

    accum[...] = jnp.zeros_like(accum)
    total[...] = jnp.zeros_like(total)
    peak[...] = jnp.full_like(peak, -FAR)

    def pass_on(i):
        above_copy(i).wait_recv()

        @pl.when(column >= 2)
        def _():
            across_copy(i, True).start()

    for i in range(PASS_ON[0][0]):
        pass_on(i)
    noisy_local(0).wait()
    for k in others:
        noisy_copy(0, k).wait_recv()
    for h in range(heads_here):
        query_copy(h).start()
    for which in (1, 2):
        for k in others:
            noisy_copy(which, k).start()

    def attend(slot, whose, h, keep, at):
        lane = pl.ds(pl.multiple_of(h * HEAD_DIM, HEAD_DIM), HEAD_DIM)
        scores = lax.dot_general(
            keyval[slot, 0, :, lane], query[whose, at, lane], (((1,), (1,)), ((), ())),
            preferred_element_type=jnp.float32,
        )
        before = peak[whose, h, :, at]
        largest = jnp.where(keep, jnp.max(scores, axis=0, keepdims=True), -FAR)
        now = jnp.maximum(before, largest)
        expo = jnp.exp2((scores - jnp.where(keep, now, FAR)) * EXP2_SCALE)
        factor = jnp.exp2((before - now) * EXP2_SCALE)
        added = lax.dot_general(
            keyval[slot, 1, :, lane], expo.astype(jnp.bfloat16), (((0,), (0,)), ((), ())),
            preferred_element_type=jnp.float32,
        )
        peak[whose, h, :, at] = now
        total[whose, h, :, at] = total[whose, h, :, at] * factor + jnp.sum(expo, axis=0, keepdims=True)
        accum[whose, h, :, at] = accum[whose, h, :, at] * factor + added

    every = pl.ds(0, tokens)

    def tile_of(t):
        return pl.ds(t * (tokens // TILES), tokens // TILES)

    def merge(h, tile=None):
        at = every if tile is None else tile_of(tile)
        for copy in part_copies(h, tile):
            copy.wait_recv()
        here, there = peak[MINE, h, :, at], got_stat[h, 0:1, at]
        now = jnp.maximum(here, there)
        a = jnp.exp2((here - now) * EXP2_SCALE)
        b = jnp.exp2((there - now) * EXP2_SCALE)
        inverse = 1.0 / (total[MINE, h, :, at] * a + got_stat[h, 1:2, at] * b)
        summed = accum[MINE, h, :, at] * (a * inverse) + got[h, :, at].astype(jnp.float32) * (b * inverse)
        final[h, at, :] = jnp.transpose(summed).astype(final.dtype)
        for j in range(at.start // rows, (at.start + at.size) // rows):

            @pl.when(head != j)
            def _():
                out_copy(h, j).start()

            @pl.when(head == j)
            def _():
                out_local(h).start()

    def hand_over(h, tile=None):
        at = every if tile is None else tile_of(tile)
        part[h, :, at] = accum[PARTNER, h, :, at].astype(part.dtype)
        part_stat[h, 0:1, at] = peak[PARTNER, h, :, at]
        part_stat[h, 1:2, at] = total[PARTNER, h, :, at]
        for copy in part_copies(h, tile):
            copy.start()

    def take_across(h):
        for i in pieces:
            if i // (2 * SPLIT) == h:
                across_copy(i, False).wait_recv()

    def take_noisy():
        for which in (1, 2):
            noisy_local(which).wait()
            for k in others:
                noisy_copy(which, k).wait_recv()

    hooks = {}
    seen = set()
    for i, (slot, whose, h) in enumerate(STEPS):
        todo = hooks.setdefault(i, [])
        for j in PASS_ON.get(i, ()):
            todo.append(functools.partial(pass_on, j))
        if whose == PARTNER and ("query", h) not in seen:
            seen.add(("query", h))
            todo.append(functools.partial(lambda h: query_copy(h).wait_recv(), h))
        if slot == ACROSS and ("across", h) not in seen:
            seen.add(("across", h))
            todo.append(functools.partial(take_across, h))
        if slot == NOISY and "noisy" not in seen:
            seen.add("noisy")
            todo.append(take_noisy)
    after = {}
    for i, h in HAND_OVER_AFTER.items():
        after.setdefault(i, []).append(functools.partial(hand_over, h))
    for i, h in MERGE_AFTER.items():
        after.setdefault(i, []).append(functools.partial(merge, h))

    def distance(slot, whose, is_odd):
        if slot == NOISY:
            return -1
        if whose == MINE:
            return 3 if slot == ABOVE else (2 if is_odd else 0)
        return 1 if slot == ACROSS else (2 if is_odd else 0)

    def one(step, carry):
        for i, todo in hooks.items():
            if todo:

                @pl.when(step == i)
                def _():
                    for act in todo:
                        act()

        shared = jnp.where(odd == 1, ABOVE, OWN)
        slot = lookup(step, [-1 if s is None else s for s, _, _ in STEPS])
        slot = jnp.where(slot < 0, shared, slot)
        whose = lookup(step, [w for _, w, _ in STEPS])
        h = lookup(step, [h for _, _, h in STEPS])
        at = jnp.where(
            odd == 1,
            lookup(step, [distance(s, w, True) for s, w, _ in STEPS]),
            lookup(step, [distance(s, w, False) for s, w, _ in STEPS]),
        )
        keep = at < 0
        for j in range(REACH):
            keep = keep | ((at == j) & jnp.where(whose == MINE, mine_ok[j], near_ok[j]))
        attend(slot, whose, h, keep, every)
        for i, todo in after.items():

            @pl.when(step == i)
            def _():
                for act in todo:
                    act()

        return carry

    lax.fori_loop(0, len(STEPS), one, 0)

    last = heads_here - 1
    take_across(last)
    for tile in range(TILES):
        attend(ACROSS, PARTNER, last, near_ok[1], tile_of(tile))
        hand_over(last, tile)
    merge(1)
    attend(ACROSS, MINE, last, (mine_ok[0] & (odd == 0)) | (mine_ok[2] & (odd == 1)), every)
    for tile in range(TILES):
        merge(last, tile)

    for h in range(heads_here):
        out_local(h).wait()
        query_copy(h).wait_send()
        for copy in [c for t in range(TILES) for c in part_copies(h, t)] if h == last else part_copies(h):
            copy.wait_send()
        for k in others:
            out_copy(h, peers[k]).wait()
            noisy_copy(h, k).wait_send()
    for i in pieces:
        above_copy(i).wait_send()
        across_copy(i, False).wait_send()


def on_device(groups, heads_axis, noisy_qkv, clean_kv, video_lengths, pattern):
    noisy = jnp.transpose(noisy_qkv, (1, 0, 2))
    tokens, _, width = clean_kv.shape
    heads_here = width // HEAD_DIM
    clean = jnp.transpose(clean_kv.reshape(tokens, 2, heads_here, HEAD_DIM), (0, 2, 1, 3))
    rows, features = noisy.shape[1:]
    dma = pltpu.SemaphoreType.DMA
    peers = heads_axis - 1
    flops = 2 * 2 * tokens * tokens * width * (REACH + 1)
    return pl.pallas_call(
        functools.partial(kernel, groups, heads_axis),
        out_shape=jax.ShapeDtypeStruct((rows, features), noisy.dtype),
        in_specs=[pl.BlockSpec(memory_space=pl.ANY)] * 2 + [pl.BlockSpec(memory_space=pltpu.SMEM)] * 2,
        out_specs=pl.BlockSpec(memory_space=pl.ANY),
        scratch_shapes=[
            pltpu.VMEM((heads_here, tokens, 2, HEAD_DIM), noisy.dtype),
            pltpu.VMEM((2, tokens, width), noisy.dtype),
            pltpu.VMEM((4, 2, tokens, width), noisy.dtype),
            pltpu.VMEM((2, heads_here, HEAD_DIM, tokens), jnp.float32),
            pltpu.VMEM((2, heads_here, 1, tokens), jnp.float32),
            pltpu.VMEM((2, heads_here, 1, tokens), jnp.float32),
            pltpu.VMEM((heads_here, HEAD_DIM, tokens), noisy.dtype),
            pltpu.VMEM((heads_here, 2, tokens), jnp.float32),
            pltpu.VMEM((heads_here, HEAD_DIM, tokens), noisy.dtype),
            pltpu.VMEM((heads_here, 2, tokens), jnp.float32),
            pltpu.VMEM((heads_here, tokens, HEAD_DIM), noisy.dtype),
            dma((3, peers)), dma((3, peers)),
            dma((2, heads_here * 2 * SPLIT)), dma((2, heads_here * 2 * SPLIT)),
            dma((heads_here,)), dma((heads_here,)),
            dma((heads_here - 1 + TILES, 2)), dma((heads_here - 1 + TILES, 2)),
            dma((heads_here, heads_axis)), dma((heads_here, heads_axis)),
            dma((3 + 2 * heads_here,)),
        ],
        compiler_params=pltpu.CompilerParams(
            collective_id=0, has_side_effects=True, vmem_limit_bytes=56 * 2**20
        ),
        cost_estimate=pl.CostEstimate(
            flops=flops, bytes_accessed=8 * tokens * width, transcendentals=tokens * tokens * heads_here * (REACH + 1)
        ),
    )(noisy, clean, video_lengths, pattern)


def solution(mesh):
    groups, heads_axis = mesh.shape["group"], mesh.shape["head"]
    return jax.shard_map(
        functools.partial(on_device, groups, heads_axis),
        mesh=mesh,
        in_specs=(P(("group", "head"), None, None), P("group", None, "head"), P(), P()),
        out_specs=P(("group", "head"), None),
        check_vma=False,
    )
```

```python
import functools

import jax
import jax.numpy as jnp
from jax import lax
from jax.experimental import pallas as pl
from jax.experimental.pallas import tpu as pltpu
from jax.sharding import PartitionSpec as P

MESH = pl.DeviceIdType.MESH
HEAD_DIM = 128
REACH = 4
ROW = 4
EXP2_SCALE = HEAD_DIM ** (-0.5) * 1.4426950408889634
FAR = 1e30

NOISY, OWN, ABOVE, ACROSS = 0, 1, 2, 3
MINE, PARTNER = 0, 1

SPLIT = 2
TILES = 4

STEPS = (
    (ABOVE, MINE, 0),
    (ACROSS, MINE, 0),
    (None, PARTNER, 0),
    (ACROSS, PARTNER, 0),
    (ABOVE, MINE, 1),
    (None, PARTNER, 1),
    (NOISY, MINE, 0),
    (ACROSS, PARTNER, 1),
    (ACROSS, MINE, 1),
    (NOISY, MINE, 1),
    (NOISY, MINE, 2),
    (None, PARTNER, 2),
    (ACROSS, PARTNER, 2),
)
PASS_ON = {0: (2, 3), 1: (4,), 3: (5,), 4: (6, 7), 5: (8,), 7: (9,), 8: (10,), 11: (11,)}
HAND_OVER_AFTER = {3: 0, 7: 1}
MERGE_AFTER = {9: 0}


def lookup(step, values):
    out = jnp.int32(values[0])
    for i, value in enumerate(values):
        if i and value != values[0]:
            out = jnp.where(step == i, jnp.int32(value), out)
    return out


def validity(group, lengths_ref, pattern_ref):
    videos = lengths_ref.shape[0]
    video, end = jnp.int32(0), jnp.int32(0)
    starts = []
    for j in range(videos):
        starts.append(end)
        end = end + lengths_ref[j]
        video = video + jnp.where(end <= group, 1, 0)
    first = jnp.int32(0)
    row = [jnp.int32(0)] * REACH
    for j in range(videos):
        first = jnp.where(video == j, starts[j], first)
        row = [jnp.where(video == j, pattern_ref[j, h], row[h]) for h in range(REACH)]
    return [(group - (h + 1) >= first) & (row[h] == 1) for h in range(REACH)]


def kernel(
    groups, heads_axis,
    noisy_ref, clean_ref, lengths_ref, pattern_ref, out_ref,
    paired, query, keyval, accum, peak, total, part, part_stat, got, got_stat, final, even_scores, odd_scores, weights,
    noisy_send, noisy_recv, clean_send, clean_recv, query_send, query_recv,
    part_send, part_recv, out_send, out_recv, local_sem,
):
    group, head = lax.axis_index("group"), lax.axis_index("head")
    rows = noisy_ref.shape[1]
    tokens, width = query.shape[1:]
    heads_here = width // HEAD_DIM
    column = lax.rem(group, ROW)
    odd = lax.rem(column, 2)
    near = group + 1 - 2 * odd
    far = group - column + (ROW - 1) - column
    below = lax.rem(group + ROW, groups)
    above = lax.rem(group + groups - ROW, groups)
    peers = [lax.rem(head + k, heads_axis) for k in range(1, heads_axis)]

    mine_ok = validity(group, lengths_ref, pattern_ref)
    near_ok = validity(near, lengths_ref, pattern_ref)

    def remote(src, dst, send, recv, to_group, to_head):
        return pltpu.make_async_remote_copy(
            src_ref=src, dst_ref=dst, send_sem=send, recv_sem=recv,
            device_id=(to_group, to_head), device_id_type=MESH,
        )

    def columns(index):
        return pl.ds(pl.multiple_of(index * width, width), width)

    def lanes(h):
        return pl.ds(h * HEAD_DIM, HEAD_DIM)

    my_rows = pl.ds(pl.multiple_of(head * rows, rows), rows)

    def noisy_target(which):
        return query.at[MINE] if which == 0 else keyval.at[NOISY, which - 1]

    def noisy_copy(which, k):
        to = peers[k]
        return remote(
            noisy_ref.at[which, :, columns(to)], noisy_target(which).at[my_rows, :],
            noisy_send.at[which, k], noisy_recv.at[which, k], group, to,
        )

    def noisy_local(which):
        return pltpu.make_async_copy(
            noisy_ref.at[which, :, columns(head)], noisy_target(which).at[my_rows, :], local_sem.at[which]
        )

    def paired_copy(h):
        return pltpu.make_async_copy(clean_ref.at[:, h], paired.at[h], local_sem.at[3 + h])

    def part_pairs(h):
        n = 2 * HEAD_DIM
        rows_of = paired.at[h].reshape(2 * tokens, HEAD_DIM)
        to, source = (lax.broadcasted_iota(jnp.int32, (n, n), axis) for axis in (0, 1))
        pick = source == 2 * lax.rem(to, HEAD_DIM) + to // HEAD_DIM
        pick = jnp.where(pick, 1.0, 0.0).astype(keyval.dtype)
        for i in range(2 * tokens // n):
            moved = jnp.dot(pick, rows_of[pl.ds(i * n, n), :], preferred_element_type=jnp.float32)
            moved = moved.astype(keyval.dtype)
            for which in range(2):
                keyval[OWN, which, pl.ds(i * HEAD_DIM, HEAD_DIM), lanes(h)] = moved[which * HEAD_DIM:(which + 1) * HEAD_DIM]

    def piece(i):
        h, rest = divmod(i, 2 * SPLIT)
        which, part_of = divmod(rest, SPLIT)
        n = keyval.shape[2] // SPLIT
        return which, pl.ds(part_of * n, n), lanes(h)

    pieces = range(heads_here * 2 * SPLIT)

    def above_copy(i):
        at = piece(i)
        return remote(
            keyval.at[(OWN, *at)], keyval.at[(ABOVE, *at)], clean_send.at[0, i], clean_recv.at[0, i], below, head
        )

    def across_copy(i, relay):
        at = piece(i)
        src = keyval.at[(ABOVE if relay else OWN, *at)]
        return remote(src, keyval.at[(ACROSS, *at)], clean_send.at[1, i], clean_recv.at[1, i], far, head)

    def query_copy(h):
        return remote(
            query.at[MINE, :, lanes(h)], query.at[PARTNER, :, lanes(h)],
            query_send.at[h], query_recv.at[h], near, head,
        )

    def part_copies(h, tile=None):
        at = pl.ds(0, tokens) if tile is None else pl.ds(tile * (tokens // TILES), tokens // TILES)
        sem = h if tile is None else h + tile
        return (
            remote(part.at[h, :, at], got.at[h, :, at], part_send.at[sem, 0], part_recv.at[sem, 0], near, head),
            remote(
                part_stat.at[h, :, at], got_stat.at[h, :, at], part_send.at[sem, 1], part_recv.at[sem, 1], near, head
            ),
        )

    def out_columns(h):
        return pl.ds(pl.multiple_of((head * heads_here + h) * HEAD_DIM, HEAD_DIM), HEAD_DIM)

    def out_copy(h, to):
        k = lax.rem(to - head + heads_axis, heads_axis)
        return remote(
            final.at[h, pl.ds(pl.multiple_of(to * rows, rows), rows), :], out_ref.at[:, out_columns(h)],
            out_send.at[h, k], out_recv.at[h, k], group, to,
        )

    def out_local(h):
        return pltpu.make_async_copy(final.at[h, my_rows, :], out_ref.at[:, out_columns(h)], local_sem.at[3 + heads_here + h])

    barrier = pltpu.get_barrier_semaphore()
    for to in peers:
        pl.semaphore_signal(barrier, inc=1, device_id=(group, to), device_id_type=MESH)
    for to in (near, far, below, above):
        pl.semaphore_signal(barrier, inc=1, device_id=(to, head), device_id_type=MESH)
    for h in range(heads_here):
        paired_copy(h).start()
    for which in range(3):
        noisy_local(which).start()
    others = range(len(peers))
    for h in range(heads_here):
        paired_copy(h).wait()
        part_pairs(h)
        if h == 0:
            pl.semaphore_wait(barrier, len(peers) + 4)
            for k in others:
                noisy_copy(0, k).start()
        for i in pieces:
            if i // (2 * SPLIT) == h:
                above_copy(i).start()

                @pl.when(column < 2)
                def _():
                    across_copy(i, False).start()

    accum[...] = jnp.zeros_like(accum)
    total[...] = jnp.zeros_like(total)
    peak[...] = jnp.full_like(peak, -FAR)

    def pass_on(i):
        above_copy(i).wait_recv()

        @pl.when(column >= 2)
        def _():
            across_copy(i, True).start()

    for i in range(PASS_ON[0][0]):
        pass_on(i)
    noisy_local(0).wait()
    for k in others:
        noisy_copy(0, k).wait_recv()
    for h in range(heads_here):
        query_copy(h).start()
    for which in (1, 2):
        for k in others:
            noisy_copy(which, k).start()

    def lane_of(h):
        return pl.ds(pl.multiple_of(h * HEAD_DIM, HEAD_DIM), HEAD_DIM)

    def score(slot, whose, h, at):
        return lax.dot_general(
            keyval[slot, 0, :, lane_of(h)], query[whose, at, lane_of(h)], (((1,), (1,)), ((), ())),
            preferred_element_type=jnp.float32,
        )

    def weigh(slot, whose, h, keep, at, scores, largest):
        before = peak[whose, h, :, at]
        now = jnp.maximum(before, jnp.where(keep, largest, -FAR))
        expo = jnp.exp2((scores - jnp.where(keep, now, FAR)) * EXP2_SCALE)
        factor = jnp.exp2((before - now) * EXP2_SCALE)
        added = lax.dot_general(
            keyval[slot, 1, :, lane_of(h)], expo.astype(jnp.bfloat16), (((0,), (0,)), ((), ())),
            preferred_element_type=jnp.float32,
        )
        peak[whose, h, :, at] = now
        total[whose, h, :, at] = total[whose, h, :, at] * factor + jnp.sum(expo, axis=0, keepdims=True)
        accum[whose, h, :, at] = accum[whose, h, :, at] * factor + added

    def attend(slot, whose, h, keep, at):
        scores = score(slot, whose, h, at)
        weigh(slot, whose, h, keep, at, scores, jnp.max(scores, axis=0, keepdims=True))

    every = pl.ds(0, tokens)

    def tile_of(t):
        return pl.ds(t * (tokens // TILES), tokens // TILES)

    def merge(h, tile=None):
        at = every if tile is None else tile_of(tile)
        for copy in part_copies(h, tile):
            copy.wait_recv()
        here, there = peak[MINE, h, :, at], got_stat[h, 0:1, at]
        now = jnp.maximum(here, there)
        a = jnp.exp2((here - now) * EXP2_SCALE)
        b = jnp.exp2((there - now) * EXP2_SCALE)
        inverse = 1.0 / (total[MINE, h, :, at] * a + got_stat[h, 1:2, at] * b)
        summed = accum[MINE, h, :, at] * (a * inverse) + got[h, :, at].astype(jnp.float32) * (b * inverse)
        final[h, at, :] = jnp.transpose(summed).astype(final.dtype)
        for j in range(at.start // rows, (at.start + at.size) // rows):

            @pl.when(head != j)
            def _():
                out_copy(h, j).start()

            @pl.when(head == j)
            def _():
                out_local(h).start()

    def hand_over(h, tile=None):
        at = every if tile is None else tile_of(tile)
        part[h, :, at] = accum[PARTNER, h, :, at].astype(part.dtype)
        part_stat[h, 0:1, at] = peak[PARTNER, h, :, at]
        part_stat[h, 1:2, at] = total[PARTNER, h, :, at]
        for copy in part_copies(h, tile):
            copy.start()

    def take_across(h, which=None):
        for i in pieces:
            if i // (2 * SPLIT) == h and which in (None, i // SPLIT % 2):
                across_copy(i, False).wait_recv()

    def take_noisy():
        for which in (1, 2):
            noisy_local(which).wait()
            for k in others:
                noisy_copy(which, k).wait_recv()

    hooks = {}
    seen = set()
    for i, (slot, whose, h) in enumerate(STEPS[:-1]):
        todo = hooks.setdefault(i, [])
        for j in PASS_ON.get(i, ()):
            todo.append(functools.partial(pass_on, j))
        if whose == PARTNER and ("query", h) not in seen:
            seen.add(("query", h))
            todo.append(functools.partial(lambda h: query_copy(h).wait_recv(), h))
        if slot == ACROSS and ("across", h) not in seen:
            seen.add(("across", h))
            todo.append(functools.partial(take_across, h))
        if slot == NOISY and "noisy" not in seen:
            seen.add("noisy")
            todo.append(take_noisy)
    after = {}
    for i, h in HAND_OVER_AFTER.items():
        after.setdefault(i, []).append(functools.partial(hand_over, h))
    for i, h in MERGE_AFTER.items():
        after.setdefault(i, []).append(functools.partial(merge, h))

    def distance(slot, whose, is_odd):
        if slot == NOISY:
            return -1
        if whose == MINE:
            return 3 if slot == ABOVE else (2 if is_odd else 0)
        return 1 if slot == ACROSS else (2 if is_odd else 0)

    def run(actions, step, parity):
        for i, todo in actions.items():
            if todo and i % 2 == parity:

                @pl.when(step == i)
                def _():
                    for act in todo:
                        act()

    def operands(step):
        shared = jnp.where(odd == 1, ABOVE, OWN)
        slot = lookup(step, [-1 if s is None else s for s, _, _ in STEPS])
        slot = jnp.where(slot < 0, shared, slot)
        return slot, lookup(step, [w for _, w, _ in STEPS]), lookup(step, [h for _, _, h in STEPS])

    def kept(step, whose):
        at = jnp.where(
            odd == 1,
            lookup(step, [distance(s, w, True) for s, w, _ in STEPS]),
            lookup(step, [distance(s, w, False) for s, w, _ in STEPS]),
        )
        keep = at < 0
        for j in range(REACH):
            keep = keep | ((at == j) & jnp.where(whose == MINE, mine_ok[j], near_ok[j]))
        return keep

    def begin(step, held):
        return begin_at(*operands(step), held)

    def begin_at(slot, whose, h, held):
        scores = score(slot, whose, h, every)
        held[...] = scores
        return jnp.max(scores, axis=0, keepdims=True)

    def finish(step, held, largest):
        slot, whose, h = operands(step)
        weigh(slot, whose, h, kept(step, whose), every, held[...], largest)

    def two(pair, largest):
        step = 2 * pair
        run(hooks, step + 1, 1)
        following = begin(step + 1, odd_scores)
        finish(step, even_scores, largest)
        run(after, step, 0)
        run(hooks, step + 2, 0)
        largest = begin(step + 2, even_scores)
        finish(step + 1, odd_scores, following)
        run(after, step + 1, 1)
        return largest

    for act in hooks.pop(0):
        act()
    largest = begin(0, even_scores)
    final_steps = len(STEPS) - 2
    largest = lax.fori_loop(0, final_steps // 2, two, largest)

    last = heads_here - 1
    for act in hooks.pop(final_steps):
        act()
    following = begin(final_steps, odd_scores)
    finish(final_steps - 1, even_scores, largest)
    take_across(last, 0)
    largest = begin(final_steps + 1, even_scores)
    finish(final_steps, odd_scores, following)

    before = peak[PARTNER, last]
    now = jnp.maximum(before, jnp.where(near_ok[1], largest, -FAR))
    expo = jnp.exp2((even_scores[...] - jnp.where(near_ok[1], now, FAR)) * EXP2_SCALE)
    factor = jnp.exp2((before - now) * EXP2_SCALE)
    weights[...] = expo.astype(weights.dtype)
    peak[PARTNER, last] = now
    total[PARTNER, last] = total[PARTNER, last] * factor + jnp.sum(expo, axis=0, keepdims=True)
    following = begin_at(ABOVE, MINE, last, odd_scores)
    take_across(last, 1)
    for tile in range(TILES):
        at = tile_of(tile)
        added = lax.dot_general(
            keyval[ACROSS, 1, :, lanes(last)], weights[:, at], (((0,), (0,)), ((), ())),
            preferred_element_type=jnp.float32,
        )
        n = tokens // TILES
        accum[PARTNER, last, :, at] = accum[PARTNER, last, :, at] * factor[:, tile * n:(tile + 1) * n] + added
        hand_over(last, tile)
    largest = begin_at(ACROSS, MINE, last, even_scores)
    weigh(ABOVE, MINE, last, mine_ok[3], every, odd_scores[...], following)
    merge(1)
    keep = (mine_ok[0] & (odd == 0)) | (mine_ok[2] & (odd == 1))
    weigh(ACROSS, MINE, last, keep, every, even_scores[...], largest)
    for tile in range(TILES):
        merge(last, tile)

    for h in range(heads_here):
        out_local(h).wait()
        query_copy(h).wait_send()
        for copy in [c for t in range(TILES) for c in part_copies(h, t)] if h == last else part_copies(h):
            copy.wait_send()
        for k in others:
            out_copy(h, peers[k]).wait()
            noisy_copy(h, k).wait_send()
    for i in pieces:
        above_copy(i).wait_send()
        across_copy(i, False).wait_send()


def on_device(groups, heads_axis, noisy_qkv, clean_kv, video_lengths, pattern):
    noisy = jnp.transpose(noisy_qkv, (1, 0, 2))
    tokens, _, width = clean_kv.shape
    heads_here = width // HEAD_DIM
    clean = jnp.transpose(clean_kv.reshape(tokens, 2, heads_here, HEAD_DIM), (0, 2, 1, 3))
    rows, features = noisy.shape[1:]
    dma = pltpu.SemaphoreType.DMA
    peers = heads_axis - 1
    flops = 2 * 2 * tokens * tokens * width * (REACH + 1)
    return pl.pallas_call(
        functools.partial(kernel, groups, heads_axis),
        out_shape=jax.ShapeDtypeStruct((rows, features), noisy.dtype),
        in_specs=[pl.BlockSpec(memory_space=pl.ANY)] * 2 + [pl.BlockSpec(memory_space=pltpu.SMEM)] * 2,
        out_specs=pl.BlockSpec(memory_space=pl.ANY),
        scratch_shapes=[
            pltpu.VMEM((heads_here, tokens, 2, HEAD_DIM), noisy.dtype),
            pltpu.VMEM((2, tokens, width), noisy.dtype),
            pltpu.VMEM((4, 2, tokens, width), noisy.dtype),
            pltpu.VMEM((2, heads_here, HEAD_DIM, tokens), jnp.float32),
            pltpu.VMEM((2, heads_here, 1, tokens), jnp.float32),
            pltpu.VMEM((2, heads_here, 1, tokens), jnp.float32),
            pltpu.VMEM((heads_here, HEAD_DIM, tokens), noisy.dtype),
            pltpu.VMEM((heads_here, 2, tokens), jnp.float32),
            pltpu.VMEM((heads_here, HEAD_DIM, tokens), noisy.dtype),
            pltpu.VMEM((heads_here, 2, tokens), jnp.float32),
            pltpu.VMEM((heads_here, tokens, HEAD_DIM), noisy.dtype),
            pltpu.VMEM((tokens, tokens), jnp.float32),
            pltpu.VMEM((tokens, tokens), jnp.float32),
            pltpu.VMEM((tokens, tokens), noisy.dtype),
            dma((3, peers)), dma((3, peers)),
            dma((2, heads_here * 2 * SPLIT)), dma((2, heads_here * 2 * SPLIT)),
            dma((heads_here,)), dma((heads_here,)),
            dma((heads_here - 1 + TILES, 2)), dma((heads_here - 1 + TILES, 2)),
            dma((heads_here, heads_axis)), dma((heads_here, heads_axis)),
            dma((3 + 2 * heads_here,)),
        ],
        compiler_params=pltpu.CompilerParams(
            collective_id=0, has_side_effects=True, vmem_limit_bytes=56 * 2**20
        ),
        cost_estimate=pl.CostEstimate(
            flops=flops, bytes_accessed=8 * tokens * width, transcendentals=tokens * tokens * heads_here * (REACH + 1)
        ),
    )(noisy, clean, video_lengths, pattern)


def solution(mesh):
    groups, heads_axis = mesh.shape["group"], mesh.shape["head"]
    return jax.shard_map(
        functools.partial(on_device, groups, heads_axis),
        mesh=mesh,
        in_specs=(P(("group", "head"), None, None), P("group", None, "head"), P(), P()),
        out_specs=P(("group", "head"), None),
        check_vma=False,
    )
```

```python
import functools

import jax
import jax.numpy as jnp
from jax import lax
from jax.experimental import pallas as pl
from jax.experimental.pallas import tpu as pltpu
from jax.sharding import PartitionSpec as P

MESH = pl.DeviceIdType.MESH
HEAD_DIM = 128
REACH = 4
ROW = 4
EXP2_SCALE = HEAD_DIM ** (-0.5) * 1.4426950408889634
FAR = 1e30

NOISY, OWN, ABOVE, ACROSS = 0, 1, 2, 3
MINE, PARTNER = 0, 1

SPLIT = 2
TILES = 4

STEPS = (
    (ABOVE, MINE, 0),
    (ACROSS, MINE, 0),
    (None, PARTNER, 0),
    (ACROSS, PARTNER, 0),
    (ABOVE, MINE, 1),
    (None, PARTNER, 1),
    (NOISY, MINE, 0),
    (ACROSS, PARTNER, 1),
    (ACROSS, MINE, 1),
    (NOISY, MINE, 1),
    (NOISY, MINE, 2),
    (None, PARTNER, 2),
    (ACROSS, PARTNER, 2),
)
PASS_ON = {0: (2, 3), 1: (4,), 3: (5,), 4: (6, 7), 5: (8,), 7: (9,), 8: (10,), 11: (11,)}
HAND_OVER_AFTER = {3: 0, 7: 1}
MERGE_AFTER = {9: 0}


def lookup(step, values):
    out = jnp.int32(values[0])
    for i, value in enumerate(values):
        if i and value != values[0]:
            out = jnp.where(step == i, jnp.int32(value), out)
    return out


def validity(group, lengths_ref, pattern_ref):
    videos = lengths_ref.shape[0]
    video, end = jnp.int32(0), jnp.int32(0)
    starts = []
    for j in range(videos):
        starts.append(end)
        end = end + lengths_ref[j]
        video = video + jnp.where(end <= group, 1, 0)
    first = jnp.int32(0)
    row = [jnp.int32(0)] * REACH
    for j in range(videos):
        first = jnp.where(video == j, starts[j], first)
        row = [jnp.where(video == j, pattern_ref[j, h], row[h]) for h in range(REACH)]
    return [(group - (h + 1) >= first) & (row[h] == 1) for h in range(REACH)]


def kernel(
    groups, heads_axis,
    noisy_ref, clean_ref, lengths_ref, pattern_ref, out_ref,
    paired, query, keyval, accum, peak, total, part, part_stat, got, got_stat, final, even_scores, odd_scores, weights,
    noisy_send, noisy_recv, clean_send, clean_recv, query_send, query_recv,
    part_send, part_recv, out_send, out_recv, local_sem,
):
    group, head = lax.axis_index("group"), lax.axis_index("head")
    rows = noisy_ref.shape[1]
    tokens, width = query.shape[1:]
    heads_here = width // HEAD_DIM
    column = lax.rem(group, ROW)
    odd = lax.rem(column, 2)
    near = group + 1 - 2 * odd
    far = group - column + (ROW - 1) - column
    below = lax.rem(group + ROW, groups)
    above = lax.rem(group + groups - ROW, groups)
    first_row, sends_below = group < ROW, group < groups - ROW
    peers = [lax.rem(head + k, heads_axis) for k in range(1, heads_axis)]

    mine_ok = validity(group, lengths_ref, pattern_ref)
    near_ok = validity(near, lengths_ref, pattern_ref)

    def remote(src, dst, send, recv, to_group, to_head):
        return pltpu.make_async_remote_copy(
            src_ref=src, dst_ref=dst, send_sem=send, recv_sem=recv,
            device_id=(to_group, to_head), device_id_type=MESH,
        )

    def columns(index):
        return pl.ds(pl.multiple_of(index * width, width), width)

    def lanes(h):
        return pl.ds(h * HEAD_DIM, HEAD_DIM)

    my_rows = pl.ds(pl.multiple_of(head * rows, rows), rows)

    def noisy_target(which):
        return query.at[MINE] if which == 0 else keyval.at[NOISY, which - 1]

    def noisy_copy(which, k):
        to = peers[k]
        return remote(
            noisy_ref.at[which, :, columns(to)], noisy_target(which).at[my_rows, :],
            noisy_send.at[which, k], noisy_recv.at[which, k], group, to,
        )

    def noisy_local(which):
        return pltpu.make_async_copy(
            noisy_ref.at[which, :, columns(head)], noisy_target(which).at[my_rows, :], local_sem.at[which]
        )

    def paired_copy(h):
        return pltpu.make_async_copy(clean_ref.at[:, h], paired.at[h], local_sem.at[3 + h])

    def part_pairs(h):
        n = 2 * HEAD_DIM
        rows_of = paired.at[h].reshape(2 * tokens, HEAD_DIM)
        to, source = (lax.broadcasted_iota(jnp.int32, (n, n), axis) for axis in (0, 1))
        pick = source == 2 * lax.rem(to, HEAD_DIM) + to // HEAD_DIM
        pick = jnp.where(pick, 1.0, 0.0).astype(keyval.dtype)
        for i in range(2 * tokens // n):
            moved = jnp.dot(pick, rows_of[pl.ds(i * n, n), :], preferred_element_type=jnp.float32)
            moved = moved.astype(keyval.dtype)
            for which in range(2):
                keyval[OWN, which, pl.ds(i * HEAD_DIM, HEAD_DIM), lanes(h)] = moved[which * HEAD_DIM:(which + 1) * HEAD_DIM]

    def piece(i):
        h, rest = divmod(i, 2 * SPLIT)
        which, part_of = divmod(rest, SPLIT)
        n = keyval.shape[2] // SPLIT
        return which, pl.ds(part_of * n, n), lanes(h)

    pieces = range(heads_here * 2 * SPLIT)

    def above_copy(i):
        at = piece(i)
        return remote(
            keyval.at[(OWN, *at)], keyval.at[(ABOVE, *at)], clean_send.at[0, i], clean_recv.at[0, i], below, head
        )

    def fill_copy(i):
        at = piece(i)
        return pltpu.make_async_copy(keyval.at[(OWN, *at)], keyval.at[(ABOVE, *at)], clean_recv.at[0, i])

    def across_copy(i, relay):
        at = piece(i)
        src = keyval.at[(ABOVE if relay else OWN, *at)]
        return remote(src, keyval.at[(ACROSS, *at)], clean_send.at[1, i], clean_recv.at[1, i], far, head)

    def query_copy(h):
        return remote(
            query.at[MINE, :, lanes(h)], query.at[PARTNER, :, lanes(h)],
            query_send.at[h], query_recv.at[h], near, head,
        )

    def part_copies(h, tile=None):
        at = pl.ds(0, tokens) if tile is None else pl.ds(tile * (tokens // TILES), tokens // TILES)
        sem = h if tile is None else h + tile
        return (
            remote(part.at[h, :, at], got.at[h, :, at], part_send.at[sem, 0], part_recv.at[sem, 0], near, head),
            remote(
                part_stat.at[h, :, at], got_stat.at[h, :, at], part_send.at[sem, 1], part_recv.at[sem, 1], near, head
            ),
        )

    def out_columns(h):
        return pl.ds(pl.multiple_of((head * heads_here + h) * HEAD_DIM, HEAD_DIM), HEAD_DIM)

    def out_copy(h, to):
        k = lax.rem(to - head + heads_axis, heads_axis)
        return remote(
            final.at[h, pl.ds(pl.multiple_of(to * rows, rows), rows), :], out_ref.at[:, out_columns(h)],
            out_send.at[h, k], out_recv.at[h, k], group, to,
        )

    def out_local(h):
        return pltpu.make_async_copy(final.at[h, my_rows, :], out_ref.at[:, out_columns(h)], local_sem.at[3 + heads_here + h])

    barrier = pltpu.get_barrier_semaphore()
    for to in peers:
        pl.semaphore_signal(barrier, inc=1, device_id=(group, to), device_id_type=MESH)
    for to in (near, far):
        pl.semaphore_signal(barrier, inc=1, device_id=(to, head), device_id_type=MESH)

    @pl.when(sends_below)
    def _():
        pl.semaphore_signal(barrier, inc=1, device_id=(below, head), device_id_type=MESH)

    @pl.when(~first_row)
    def _():
        pl.semaphore_signal(barrier, inc=1, device_id=(above, head), device_id_type=MESH)

    for h in range(heads_here):
        paired_copy(h).start()
    for which in range(3):
        noisy_local(which).start()
    others = range(len(peers))
    for h in range(heads_here):
        paired_copy(h).wait()
        part_pairs(h)
        if h == 0:
            pl.semaphore_wait(barrier, len(peers) + 2 + jnp.where(sends_below, 1, 0) + jnp.where(first_row, 0, 1))
            for k in others:
                noisy_copy(0, k).start()
        of_head = [i for i in pieces if i // (2 * SPLIT) == h]

        @pl.when(sends_below)
        def _():
            for i in of_head:
                above_copy(i).start()

        @pl.when(first_row)
        def _():
            for i in of_head:
                fill_copy(i).start()

        @pl.when(column < 2)
        def _():
            for i in of_head:
                across_copy(i, False).start()

    accum[...] = jnp.zeros_like(accum)
    total[...] = jnp.zeros_like(total)
    peak[...] = jnp.full_like(peak, -FAR)

    def pass_on(i):
        above_copy(i).wait_recv()

        @pl.when(column >= 2)
        def _():
            across_copy(i, True).start()

    for i in range(PASS_ON[0][0]):
        pass_on(i)
    noisy_local(0).wait()
    for k in others:
        noisy_copy(0, k).wait_recv()
    for h in range(heads_here):
        query_copy(h).start()
    for which in (1, 2):
        for k in others:
            noisy_copy(which, k).start()

    def lane_of(h):
        return pl.ds(pl.multiple_of(h * HEAD_DIM, HEAD_DIM), HEAD_DIM)

    def score(slot, whose, h, at):
        return lax.dot_general(
            keyval[slot, 0, :, lane_of(h)], query[whose, at, lane_of(h)], (((1,), (1,)), ((), ())),
            preferred_element_type=jnp.float32,
        )

    def weigh(slot, whose, h, keep, at, scores, largest):
        before = peak[whose, h, :, at]
        now = jnp.maximum(before, jnp.where(keep, largest, -FAR))
        expo = jnp.exp2((scores - jnp.where(keep, now, FAR)) * EXP2_SCALE)
        factor = jnp.exp2((before - now) * EXP2_SCALE)
        added = lax.dot_general(
            keyval[slot, 1, :, lane_of(h)], expo.astype(jnp.bfloat16), (((0,), (0,)), ((), ())),
            preferred_element_type=jnp.float32,
        )
        peak[whose, h, :, at] = now
        total[whose, h, :, at] = total[whose, h, :, at] * factor + jnp.sum(expo, axis=0, keepdims=True)
        accum[whose, h, :, at] = accum[whose, h, :, at] * factor + added

    def attend(slot, whose, h, keep, at):
        scores = score(slot, whose, h, at)
        weigh(slot, whose, h, keep, at, scores, jnp.max(scores, axis=0, keepdims=True))

    every = pl.ds(0, tokens)

    def tile_of(t):
        return pl.ds(t * (tokens // TILES), tokens // TILES)

    def merge(h, tile=None):
        at = every if tile is None else tile_of(tile)
        for copy in part_copies(h, tile):
            copy.wait_recv()
        here, there = peak[MINE, h, :, at], got_stat[h, 0:1, at]
        now = jnp.maximum(here, there)
        a = jnp.exp2((here - now) * EXP2_SCALE)
        b = jnp.exp2((there - now) * EXP2_SCALE)
        inverse = 1.0 / (total[MINE, h, :, at] * a + got_stat[h, 1:2, at] * b)
        summed = accum[MINE, h, :, at] * (a * inverse) + got[h, :, at].astype(jnp.float32) * (b * inverse)
        final[h, at, :] = jnp.transpose(summed).astype(final.dtype)
        for j in range(at.start // rows, (at.start + at.size) // rows):

            @pl.when(head != j)
            def _():
                out_copy(h, j).start()

            @pl.when(head == j)
            def _():
                out_local(h).start()

    def hand_over(h, tile=None):
        at = every if tile is None else tile_of(tile)
        part[h, :, at] = accum[PARTNER, h, :, at].astype(part.dtype)
        part_stat[h, 0:1, at] = peak[PARTNER, h, :, at]
        part_stat[h, 1:2, at] = total[PARTNER, h, :, at]
        for copy in part_copies(h, tile):
            copy.start()

    def take_across(h, which=None):
        for i in pieces:
            if i // (2 * SPLIT) == h and which in (None, i // SPLIT % 2):
                across_copy(i, False).wait_recv()

    def take_noisy():
        for which in (1, 2):
            noisy_local(which).wait()
            for k in others:
                noisy_copy(which, k).wait_recv()

    hooks = {}
    seen = set()
    for i, (slot, whose, h) in enumerate(STEPS[:-1]):
        todo = hooks.setdefault(i, [])
        for j in PASS_ON.get(i, ()):
            todo.append(functools.partial(pass_on, j))
        if whose == PARTNER and ("query", h) not in seen:
            seen.add(("query", h))
            todo.append(functools.partial(lambda h: query_copy(h).wait_recv(), h))
        if slot == ACROSS and ("across", h) not in seen:
            seen.add(("across", h))
            todo.append(functools.partial(take_across, h))
        if slot == NOISY and "noisy" not in seen:
            seen.add("noisy")
            todo.append(take_noisy)
    after = {}
    for i, h in HAND_OVER_AFTER.items():
        after.setdefault(i, []).append(functools.partial(hand_over, h))
    for i, h in MERGE_AFTER.items():
        after.setdefault(i, []).append(functools.partial(merge, h))

    def distance(slot, whose, is_odd):
        if slot == NOISY:
            return -1
        if whose == MINE:
            return 3 if slot == ABOVE else (2 if is_odd else 0)
        return 1 if slot == ACROSS else (2 if is_odd else 0)

    def run(actions, step, parity):
        for i, todo in actions.items():
            if todo and i % 2 == parity:

                @pl.when(step == i)
                def _():
                    for act in todo:
                        act()

    def operands(step):
        shared = jnp.where(odd == 1, ABOVE, OWN)
        slot = lookup(step, [-1 if s is None else s for s, _, _ in STEPS])
        slot = jnp.where(slot < 0, shared, slot)
        return slot, lookup(step, [w for _, w, _ in STEPS]), lookup(step, [h for _, _, h in STEPS])

    def kept(step, whose):
        at = jnp.where(
            odd == 1,
            lookup(step, [distance(s, w, True) for s, w, _ in STEPS]),
            lookup(step, [distance(s, w, False) for s, w, _ in STEPS]),
        )
        keep = at < 0
        for j in range(REACH):
            keep = keep | ((at == j) & jnp.where(whose == MINE, mine_ok[j], near_ok[j]))
        return keep

    def begin(step, held):
        return begin_at(*operands(step), held)

    def begin_at(slot, whose, h, held):
        scores = score(slot, whose, h, every)
        held[...] = scores
        return jnp.max(scores, axis=0, keepdims=True)

    def finish(step, held, largest):
        slot, whose, h = operands(step)
        weigh(slot, whose, h, kept(step, whose), every, held[...], largest)

    def two(pair, largest):
        step = 2 * pair
        run(hooks, step + 1, 1)
        following = begin(step + 1, odd_scores)
        finish(step, even_scores, largest)
        run(after, step, 0)
        run(hooks, step + 2, 0)
        largest = begin(step + 2, even_scores)
        finish(step + 1, odd_scores, following)
        run(after, step + 1, 1)
        return largest

    for act in hooks.pop(0):
        act()
    largest = begin(0, even_scores)
    final_steps = len(STEPS) - 2
    largest = lax.fori_loop(0, final_steps // 2, two, largest)

    last = heads_here - 1
    for act in hooks.pop(final_steps):
        act()
    following = begin(final_steps, odd_scores)
    finish(final_steps - 1, even_scores, largest)
    take_across(last, 0)
    largest = begin(final_steps + 1, even_scores)
    finish(final_steps, odd_scores, following)

    before = peak[PARTNER, last]
    now = jnp.maximum(before, jnp.where(near_ok[1], largest, -FAR))
    expo = jnp.exp2((even_scores[...] - jnp.where(near_ok[1], now, FAR)) * EXP2_SCALE)
    factor = jnp.exp2((before - now) * EXP2_SCALE)
    weights[...] = expo.astype(weights.dtype)
    peak[PARTNER, last] = now
    total[PARTNER, last] = total[PARTNER, last] * factor + jnp.sum(expo, axis=0, keepdims=True)
    following = begin_at(ABOVE, MINE, last, odd_scores)
    take_across(last, 1)
    for tile in range(TILES):
        at = tile_of(tile)
        added = lax.dot_general(
            keyval[ACROSS, 1, :, lanes(last)], weights[:, at], (((0,), (0,)), ((), ())),
            preferred_element_type=jnp.float32,
        )
        n = tokens // TILES
        accum[PARTNER, last, :, at] = accum[PARTNER, last, :, at] * factor[:, tile * n:(tile + 1) * n] + added
        hand_over(last, tile)
    largest = begin_at(ACROSS, MINE, last, even_scores)
    weigh(ABOVE, MINE, last, mine_ok[3], every, odd_scores[...], following)
    merge(1)
    keep = (mine_ok[0] & (odd == 0)) | (mine_ok[2] & (odd == 1))
    weigh(ACROSS, MINE, last, keep, every, even_scores[...], largest)
    for tile in range(TILES):
        merge(last, tile)

    for h in range(heads_here):
        out_local(h).wait()
        query_copy(h).wait_send()
        for copy in [c for t in range(TILES) for c in part_copies(h, t)] if h == last else part_copies(h):
            copy.wait_send()
        for k in others:
            out_copy(h, peers[k]).wait()
            noisy_copy(h, k).wait_send()
    for i in pieces:
        across_copy(i, False).wait_send()

    @pl.when(sends_below)
    def _():
        for i in pieces:
            above_copy(i).wait_send()


def on_device(groups, heads_axis, noisy_qkv, clean_kv, video_lengths, pattern):
    noisy = jnp.transpose(noisy_qkv, (1, 0, 2))
    tokens, _, width = clean_kv.shape
    heads_here = width // HEAD_DIM
    clean = jnp.transpose(clean_kv.reshape(tokens, 2, heads_here, HEAD_DIM), (0, 2, 1, 3))
    rows, features = noisy.shape[1:]
    dma = pltpu.SemaphoreType.DMA
    peers = heads_axis - 1
    flops = 2 * 2 * tokens * tokens * width * (REACH + 1)
    return pl.pallas_call(
        functools.partial(kernel, groups, heads_axis),
        out_shape=jax.ShapeDtypeStruct((rows, features), noisy.dtype),
        in_specs=[pl.BlockSpec(memory_space=pl.ANY)] * 2 + [pl.BlockSpec(memory_space=pltpu.SMEM)] * 2,
        out_specs=pl.BlockSpec(memory_space=pl.ANY),
        scratch_shapes=[
            pltpu.VMEM((heads_here, tokens, 2, HEAD_DIM), noisy.dtype),
            pltpu.VMEM((2, tokens, width), noisy.dtype),
            pltpu.VMEM((4, 2, tokens, width), noisy.dtype),
            pltpu.VMEM((2, heads_here, HEAD_DIM, tokens), jnp.float32),
            pltpu.VMEM((2, heads_here, 1, tokens), jnp.float32),
            pltpu.VMEM((2, heads_here, 1, tokens), jnp.float32),
            pltpu.VMEM((heads_here, HEAD_DIM, tokens), noisy.dtype),
            pltpu.VMEM((heads_here, 2, tokens), jnp.float32),
            pltpu.VMEM((heads_here, HEAD_DIM, tokens), noisy.dtype),
            pltpu.VMEM((heads_here, 2, tokens), jnp.float32),
            pltpu.VMEM((heads_here, tokens, HEAD_DIM), noisy.dtype),
            pltpu.VMEM((tokens, tokens), jnp.float32),
            pltpu.VMEM((tokens, tokens), jnp.float32),
            pltpu.VMEM((tokens, tokens), noisy.dtype),
            dma((3, peers)), dma((3, peers)),
            dma((2, heads_here * 2 * SPLIT)), dma((2, heads_here * 2 * SPLIT)),
            dma((heads_here,)), dma((heads_here,)),
            dma((heads_here - 1 + TILES, 2)), dma((heads_here - 1 + TILES, 2)),
            dma((heads_here, heads_axis)), dma((heads_here, heads_axis)),
            dma((3 + 2 * heads_here,)),
        ],
        compiler_params=pltpu.CompilerParams(
            collective_id=0, has_side_effects=True, vmem_limit_bytes=56 * 2**20
        ),
        cost_estimate=pl.CostEstimate(
            flops=flops, bytes_accessed=8 * tokens * width, transcendentals=tokens * tokens * heads_here * (REACH + 1)
        ),
    )(noisy, clean, video_lengths, pattern)


def solution(mesh):
    groups, heads_axis = mesh.shape["group"], mesh.shape["head"]
    return jax.shard_map(
        functools.partial(on_device, groups, heads_axis),
        mesh=mesh,
        in_specs=(P(("group", "head"), None, None), P("group", None, "head"), P(), P()),
        out_specs=P(("group", "head"), None),
        check_vma=False,
    )
```

```python
import functools

import jax
import jax.numpy as jnp
from jax import lax
from jax.experimental import pallas as pl
from jax.experimental.pallas import tpu as pltpu
from jax.sharding import PartitionSpec as P

MESH = pl.DeviceIdType.MESH
HEAD_DIM = 128
REACH = 4
ROW = 4
EXP2_SCALE = HEAD_DIM ** (-0.5) * 1.4426950408889634
FAR = 1e30

NOISY, OWN, ABOVE, ACROSS = 0, 1, 2, 3
MINE, PARTNER = 0, 1

SPLIT = 2
TILES = 4

STEPS = (
    (ABOVE, MINE, 0),
    (ACROSS, MINE, 0),
    (None, PARTNER, 0),
    (ACROSS, PARTNER, 0),
    (ABOVE, MINE, 1),
    (None, PARTNER, 1),
    (NOISY, MINE, 0),
    (ACROSS, PARTNER, 1),
    (ACROSS, MINE, 1),
    (NOISY, MINE, 1),
    (NOISY, MINE, 2),
    (None, PARTNER, 2),
    (ACROSS, PARTNER, 2),
)
PASS_ON = {0: (2, 3), 1: (4,), 3: (5,), 4: (6, 7), 5: (8,), 6: (9,), 8: (10,), 11: (11,)}
HAND_OVER_AFTER = {3: 0, 7: 1}
MERGE_AFTER = {9: 0}


def lookup(step, values):
    out = jnp.int32(values[0])
    for i, value in enumerate(values):
        if i and value != values[0]:
            out = jnp.where(step == i, jnp.int32(value), out)
    return out


def validity(group, lengths_ref, pattern_ref):
    videos = lengths_ref.shape[0]
    video, end = jnp.int32(0), jnp.int32(0)
    starts = []
    for j in range(videos):
        starts.append(end)
        end = end + lengths_ref[j]
        video = video + jnp.where(end <= group, 1, 0)
    first = jnp.int32(0)
    row = [jnp.int32(0)] * REACH
    for j in range(videos):
        first = jnp.where(video == j, starts[j], first)
        row = [jnp.where(video == j, pattern_ref[j, h], row[h]) for h in range(REACH)]
    return [(group - (h + 1) >= first) & (row[h] == 1) for h in range(REACH)]


def kernel(
    groups, heads_axis,
    noisy_ref, clean_ref, lengths_ref, pattern_ref, out_ref,
    paired, query, keyval, accum, peak, total, part, part_stat, got, got_stat, final, even_scores, odd_scores, weights,
    noisy_send, noisy_recv, clean_send, clean_recv, query_send, query_recv,
    part_send, part_recv, out_send, out_recv, local_sem,
):
    group, head = lax.axis_index("group"), lax.axis_index("head")
    rows = noisy_ref.shape[1]
    tokens, width = query.shape[1:]
    heads_here = width // HEAD_DIM
    column = lax.rem(group, ROW)
    odd = lax.rem(column, 2)
    near = group + 1 - 2 * odd
    far = group - column + (ROW - 1) - column
    below = lax.rem(group + ROW, groups)
    above = lax.rem(group + groups - ROW, groups)
    first_row, sends_below = group < ROW, group < groups - ROW
    peers = [lax.rem(head + k, heads_axis) for k in range(1, heads_axis)]

    mine_ok = validity(group, lengths_ref, pattern_ref)
    near_ok = validity(near, lengths_ref, pattern_ref)

    def remote(src, dst, send, recv, to_group, to_head):
        return pltpu.make_async_remote_copy(
            src_ref=src, dst_ref=dst, send_sem=send, recv_sem=recv,
            device_id=(to_group, to_head), device_id_type=MESH,
        )

    def columns(index):
        return pl.ds(pl.multiple_of(index * width, width), width)

    def lanes(h):
        return pl.ds(h * HEAD_DIM, HEAD_DIM)

    my_rows = pl.ds(pl.multiple_of(head * rows, rows), rows)

    def noisy_target(which):
        return query.at[MINE] if which == 0 else keyval.at[NOISY, which - 1]

    def noisy_copy(which, k):
        to = peers[k]
        return remote(
            noisy_ref.at[which, :, columns(to)], noisy_target(which).at[my_rows, :],
            noisy_send.at[which, k], noisy_recv.at[which, k], group, to,
        )

    def noisy_local(which):
        return pltpu.make_async_copy(
            noisy_ref.at[which, :, columns(head)], noisy_target(which).at[my_rows, :], local_sem.at[which]
        )

    def paired_copy(h):
        return pltpu.make_async_copy(clean_ref.at[:, h], paired.at[h], local_sem.at[3 + h])

    def part_pairs(h):
        n = 2 * HEAD_DIM
        rows_of = paired.at[h].reshape(2 * tokens, HEAD_DIM)
        to, source = (lax.broadcasted_iota(jnp.int32, (n, n), axis) for axis in (0, 1))
        pick = source == 2 * lax.rem(to, HEAD_DIM) + to // HEAD_DIM
        pick = jnp.where(pick, 1.0, 0.0).astype(keyval.dtype)
        for i in range(2 * tokens // n):
            moved = jnp.dot(pick, rows_of[pl.ds(i * n, n), :], preferred_element_type=jnp.float32)
            moved = moved.astype(keyval.dtype)
            for which in range(2):
                keyval[OWN, which, pl.ds(i * HEAD_DIM, HEAD_DIM), lanes(h)] = moved[which * HEAD_DIM:(which + 1) * HEAD_DIM]

    def piece(i):
        h, rest = divmod(i, 2 * SPLIT)
        which, part_of = divmod(rest, SPLIT)
        n = keyval.shape[2] // SPLIT
        return which, pl.ds(part_of * n, n), lanes(h)

    pieces = range(heads_here * 2 * SPLIT)

    def above_copy(i):
        at = piece(i)
        return remote(
            keyval.at[(OWN, *at)], keyval.at[(ABOVE, *at)], clean_send.at[0, i], clean_recv.at[0, i], below, head
        )

    def fill_copy(i):
        at = piece(i)
        return pltpu.make_async_copy(keyval.at[(OWN, *at)], keyval.at[(ABOVE, *at)], clean_recv.at[0, i])

    def across_copy(i, relay):
        at = piece(i)
        src = keyval.at[(ABOVE if relay else OWN, *at)]
        return remote(src, keyval.at[(ACROSS, *at)], clean_send.at[1, i], clean_recv.at[1, i], far, head)

    def query_copy(h):
        return remote(
            query.at[MINE, :, lanes(h)], query.at[PARTNER, :, lanes(h)],
            query_send.at[h], query_recv.at[h], near, head,
        )

    def part_copies(h, tile=None):
        at = pl.ds(0, tokens) if tile is None else pl.ds(tile * (tokens // TILES), tokens // TILES)
        sem = h if tile is None else h + tile
        return (
            remote(part.at[h, :, at], got.at[h, :, at], part_send.at[sem, 0], part_recv.at[sem, 0], near, head),
            remote(
                part_stat.at[h, :, at], got_stat.at[h, :, at], part_send.at[sem, 1], part_recv.at[sem, 1], near, head
            ),
        )

    def out_columns(h):
        return pl.ds(pl.multiple_of((head * heads_here + h) * HEAD_DIM, HEAD_DIM), HEAD_DIM)

    def out_copy(h, to):
        k = lax.rem(to - head + heads_axis, heads_axis)
        return remote(
            final.at[h, pl.ds(pl.multiple_of(to * rows, rows), rows), :], out_ref.at[:, out_columns(h)],
            out_send.at[h, k], out_recv.at[h, k], group, to,
        )

    def out_local(h):
        return pltpu.make_async_copy(final.at[h, my_rows, :], out_ref.at[:, out_columns(h)], local_sem.at[3 + heads_here + h])

    barrier = pltpu.get_barrier_semaphore()
    for to in peers:
        pl.semaphore_signal(barrier, inc=1, device_id=(group, to), device_id_type=MESH)
    for to in (near, far):
        pl.semaphore_signal(barrier, inc=1, device_id=(to, head), device_id_type=MESH)

    @pl.when(sends_below)
    def _():
        pl.semaphore_signal(barrier, inc=1, device_id=(below, head), device_id_type=MESH)

    @pl.when(~first_row)
    def _():
        pl.semaphore_signal(barrier, inc=1, device_id=(above, head), device_id_type=MESH)

    for h in range(heads_here):
        paired_copy(h).start()
    for which in range(3):
        noisy_local(which).start()
    others = range(len(peers))
    for h in range(heads_here):
        paired_copy(h).wait()
        part_pairs(h)
        if h == 0:
            pl.semaphore_wait(barrier, len(peers) + 2 + jnp.where(sends_below, 1, 0) + jnp.where(first_row, 0, 1))
            for k in others:
                noisy_copy(0, k).start()
        of_head = [i for i in pieces if i // (2 * SPLIT) == h]

        @pl.when(sends_below)
        def _():
            for i in of_head:
                above_copy(i).start()

        @pl.when(first_row)
        def _():
            for i in of_head:
                fill_copy(i).start()

        @pl.when(column < 2)
        def _():
            for i in of_head:
                across_copy(i, False).start()

    accum[...] = jnp.zeros_like(accum)
    total[...] = jnp.zeros_like(total)
    peak[...] = jnp.full_like(peak, -FAR)

    def pass_on(i):
        above_copy(i).wait_recv()

        @pl.when(column >= 2)
        def _():
            across_copy(i, True).start()

    for i in range(PASS_ON[0][0]):
        pass_on(i)
    noisy_local(0).wait()
    for k in others:
        noisy_copy(0, k).wait_recv()
    for h in range(heads_here):
        query_copy(h).start()
    for which in (1, 2):
        for k in others:
            noisy_copy(which, k).start()

    def lane_of(h):
        return pl.ds(pl.multiple_of(h * HEAD_DIM, HEAD_DIM), HEAD_DIM)

    def score(slot, whose, h, at):
        return lax.dot_general(
            keyval[slot, 0, :, lane_of(h)], query[whose, at, lane_of(h)], (((1,), (1,)), ((), ())),
            preferred_element_type=jnp.float32,
        )

    def weigh(slot, whose, h, keep, at, scores, largest):
        before = peak[whose, h, :, at]
        now = jnp.maximum(before, jnp.where(keep, largest, -FAR))
        expo = jnp.exp2((scores - jnp.where(keep, now, FAR)) * EXP2_SCALE)
        factor = jnp.exp2((before - now) * EXP2_SCALE)
        added = lax.dot_general(
            keyval[slot, 1, :, lane_of(h)], expo.astype(jnp.bfloat16), (((0,), (0,)), ((), ())),
            preferred_element_type=jnp.float32,
        )
        peak[whose, h, :, at] = now
        total[whose, h, :, at] = total[whose, h, :, at] * factor + jnp.sum(expo, axis=0, keepdims=True)
        accum[whose, h, :, at] = accum[whose, h, :, at] * factor + added

    def attend(slot, whose, h, keep, at):
        scores = score(slot, whose, h, at)
        weigh(slot, whose, h, keep, at, scores, jnp.max(scores, axis=0, keepdims=True))

    every = pl.ds(0, tokens)

    def tile_of(t):
        return pl.ds(t * (tokens // TILES), tokens // TILES)

    def merge(h, tile=None):
        at = every if tile is None else tile_of(tile)
        for copy in part_copies(h, tile):
            copy.wait_recv()
        here, there = peak[MINE, h, :, at], got_stat[h, 0:1, at]
        now = jnp.maximum(here, there)
        a = jnp.exp2((here - now) * EXP2_SCALE)
        b = jnp.exp2((there - now) * EXP2_SCALE)
        inverse = 1.0 / (total[MINE, h, :, at] * a + got_stat[h, 1:2, at] * b)
        summed = accum[MINE, h, :, at] * (a * inverse) + got[h, :, at].astype(jnp.float32) * (b * inverse)
        final[h, at, :] = jnp.transpose(summed).astype(final.dtype)
        for j in range(at.start // rows, (at.start + at.size) // rows):

            @pl.when(head != j)
            def _():
                out_copy(h, j).start()

            @pl.when(head == j)
            def _():
                out_local(h).start()

    def hand_over(h, tile=None):
        at = every if tile is None else tile_of(tile)
        part[h, :, at] = accum[PARTNER, h, :, at].astype(part.dtype)
        part_stat[h, 0:1, at] = peak[PARTNER, h, :, at]
        part_stat[h, 1:2, at] = total[PARTNER, h, :, at]
        for copy in part_copies(h, tile):
            copy.start()

    def take_across(h, which=None):
        for i in pieces:
            if i // (2 * SPLIT) == h and which in (None, i // SPLIT % 2):
                across_copy(i, False).wait_recv()

    def take_noisy():
        for which in (1, 2):
            noisy_local(which).wait()
            for k in others:
                noisy_copy(which, k).wait_recv()

    hooks = {}
    seen = set()
    for i, (slot, whose, h) in enumerate(STEPS[:-1]):
        todo = hooks.setdefault(i, [])
        for j in PASS_ON.get(i, ()):
            todo.append(functools.partial(pass_on, j))
        if whose == PARTNER and ("query", h) not in seen:
            seen.add(("query", h))
            todo.append(functools.partial(lambda h: query_copy(h).wait_recv(), h))
        if slot == ACROSS and ("across", h) not in seen:
            seen.add(("across", h))
            todo.append(functools.partial(take_across, h))
        if slot == NOISY and "noisy" not in seen:
            seen.add("noisy")
            todo.append(take_noisy)
    after = {}
    for i, h in HAND_OVER_AFTER.items():
        after.setdefault(i, []).append(functools.partial(hand_over, h))
    for i, h in MERGE_AFTER.items():
        after.setdefault(i, []).append(functools.partial(merge, h))

    def distance(slot, whose, is_odd):
        if slot == NOISY:
            return -1
        if whose == MINE:
            return 3 if slot == ABOVE else (2 if is_odd else 0)
        return 1 if slot == ACROSS else (2 if is_odd else 0)

    def run(actions, step, parity):
        for i, todo in actions.items():
            if todo and i % 2 == parity:

                @pl.when(step == i)
                def _():
                    for act in todo:
                        act()

    def operands(step):
        shared = jnp.where(odd == 1, ABOVE, OWN)
        slot = lookup(step, [-1 if s is None else s for s, _, _ in STEPS])
        slot = jnp.where(slot < 0, shared, slot)
        return slot, lookup(step, [w for _, w, _ in STEPS]), lookup(step, [h for _, _, h in STEPS])

    def kept(step, whose):
        at = jnp.where(
            odd == 1,
            lookup(step, [distance(s, w, True) for s, w, _ in STEPS]),
            lookup(step, [distance(s, w, False) for s, w, _ in STEPS]),
        )
        keep = at < 0
        for j in range(REACH):
            keep = keep | ((at == j) & jnp.where(whose == MINE, mine_ok[j], near_ok[j]))
        return keep

    def begin(step, held):
        return begin_at(*operands(step), held)

    def begin_at(slot, whose, h, held):
        scores = score(slot, whose, h, every)
        held[...] = scores
        return jnp.max(scores, axis=0, keepdims=True)

    def finish(step, held, largest):
        slot, whose, h = operands(step)
        weigh(slot, whose, h, kept(step, whose), every, held[...], largest)

    def two(pair, largest):
        step = 2 * pair
        run(hooks, step + 1, 1)
        following = begin(step + 1, odd_scores)
        finish(step, even_scores, largest)
        run(after, step, 0)
        run(hooks, step + 2, 0)
        largest = begin(step + 2, even_scores)
        finish(step + 1, odd_scores, following)
        run(after, step + 1, 1)
        return largest

    for act in hooks.pop(0):
        act()
    largest = begin(0, even_scores)
    final_steps = len(STEPS) - 2
    largest = lax.fori_loop(0, final_steps // 2, two, largest)

    last = heads_here - 1
    for act in hooks.pop(final_steps):
        act()
    following = begin(final_steps, odd_scores)
    finish(final_steps - 1, even_scores, largest)
    take_across(last, 0)
    largest = begin(final_steps + 1, even_scores)
    finish(final_steps, odd_scores, following)

    before = peak[PARTNER, last]
    now = jnp.maximum(before, jnp.where(near_ok[1], largest, -FAR))
    expo = jnp.exp2((even_scores[...] - jnp.where(near_ok[1], now, FAR)) * EXP2_SCALE)
    factor = jnp.exp2((before - now) * EXP2_SCALE)
    weights[...] = expo.astype(weights.dtype)
    peak[PARTNER, last] = now
    total[PARTNER, last] = total[PARTNER, last] * factor + jnp.sum(expo, axis=0, keepdims=True)
    following = begin_at(ABOVE, MINE, last, odd_scores)
    largest = begin_at(ACROSS, MINE, last, even_scores)
    take_across(last, 1)
    for tile in range(TILES):
        at = tile_of(tile)
        added = lax.dot_general(
            keyval[ACROSS, 1, :, lanes(last)], weights[:, at], (((0,), (0,)), ((), ())),
            preferred_element_type=jnp.float32,
        )
        n = tokens // TILES
        accum[PARTNER, last, :, at] = accum[PARTNER, last, :, at] * factor[:, tile * n:(tile + 1) * n] + added
        hand_over(last, tile)
    weigh(ABOVE, MINE, last, mine_ok[3], every, odd_scores[...], following)
    merge(1)
    keep = (mine_ok[0] & (odd == 0)) | (mine_ok[2] & (odd == 1))
    weigh(ACROSS, MINE, last, keep, every, even_scores[...], largest)
    for tile in range(TILES):
        merge(last, tile)

    for h in range(heads_here):
        out_local(h).wait()
        query_copy(h).wait_send()
        for copy in [c for t in range(TILES) for c in part_copies(h, t)] if h == last else part_copies(h):
            copy.wait_send()
        for k in others:
            out_copy(h, peers[k]).wait()
            noisy_copy(h, k).wait_send()
    for i in pieces:
        across_copy(i, False).wait_send()

    @pl.when(sends_below)
    def _():
        for i in pieces:
            above_copy(i).wait_send()


def on_device(groups, heads_axis, noisy_qkv, clean_kv, video_lengths, pattern):
    noisy = jnp.transpose(noisy_qkv, (1, 0, 2))
    tokens, _, width = clean_kv.shape
    heads_here = width // HEAD_DIM
    clean = jnp.transpose(clean_kv.reshape(tokens, 2, heads_here, HEAD_DIM), (0, 2, 1, 3))
    rows, features = noisy.shape[1:]
    dma = pltpu.SemaphoreType.DMA
    peers = heads_axis - 1
    flops = 2 * 2 * tokens * tokens * width * (REACH + 1)
    return pl.pallas_call(
        functools.partial(kernel, groups, heads_axis),
        out_shape=jax.ShapeDtypeStruct((rows, features), noisy.dtype),
        in_specs=[pl.BlockSpec(memory_space=pl.ANY)] * 2 + [pl.BlockSpec(memory_space=pltpu.SMEM)] * 2,
        out_specs=pl.BlockSpec(memory_space=pl.ANY),
        scratch_shapes=[
            pltpu.VMEM((heads_here, tokens, 2, HEAD_DIM), noisy.dtype),
            pltpu.VMEM((2, tokens, width), noisy.dtype),
            pltpu.VMEM((4, 2, tokens, width), noisy.dtype),
            pltpu.VMEM((2, heads_here, HEAD_DIM, tokens), jnp.float32),
            pltpu.VMEM((2, heads_here, 1, tokens), jnp.float32),
            pltpu.VMEM((2, heads_here, 1, tokens), jnp.float32),
            pltpu.VMEM((heads_here, HEAD_DIM, tokens), noisy.dtype),
            pltpu.VMEM((heads_here, 2, tokens), jnp.float32),
            pltpu.VMEM((heads_here, HEAD_DIM, tokens), noisy.dtype),
            pltpu.VMEM((heads_here, 2, tokens), jnp.float32),
            pltpu.VMEM((heads_here, tokens, HEAD_DIM), noisy.dtype),
            pltpu.VMEM((tokens, tokens), jnp.float32),
            pltpu.VMEM((tokens, tokens), jnp.float32),
            pltpu.VMEM((tokens, tokens), noisy.dtype),
            dma((3, peers)), dma((3, peers)),
            dma((2, heads_here * 2 * SPLIT)), dma((2, heads_here * 2 * SPLIT)),
            dma((heads_here,)), dma((heads_here,)),
            dma((heads_here - 1 + TILES, 2)), dma((heads_here - 1 + TILES, 2)),
            dma((heads_here, heads_axis)), dma((heads_here, heads_axis)),
            dma((3 + 2 * heads_here,)),
        ],
        compiler_params=pltpu.CompilerParams(
            collective_id=0, has_side_effects=True, vmem_limit_bytes=56 * 2**20
        ),
        cost_estimate=pl.CostEstimate(
            flops=flops, bytes_accessed=8 * tokens * width, transcendentals=tokens * tokens * heads_here * (REACH + 1)
        ),
    )(noisy, clean, video_lengths, pattern)


def solution(mesh):
    groups, heads_axis = mesh.shape["group"], mesh.shape["head"]
    return jax.shard_map(
        functools.partial(on_device, groups, heads_axis),
        mesh=mesh,
        in_specs=(P(("group", "head"), None, None), P("group", None, "head"), P(), P()),
        out_specs=P(("group", "head"), None),
        check_vma=False,
    )
```

```python
import functools

import jax
import jax.numpy as jnp
from jax import lax
from jax.experimental import pallas as pl
from jax.experimental.pallas import tpu as pltpu
from jax.sharding import PartitionSpec as P

MESH = pl.DeviceIdType.MESH
HEAD_DIM = 128
REACH = 4
ROW = 4
EXP2_SCALE = HEAD_DIM ** (-0.5) * 1.4426950408889634
FAR = 1e30

NOISY, OWN, ABOVE, ACROSS = 0, 1, 2, 3
MINE, PARTNER = 0, 1

SPLIT = 2
TILES = 4

STEPS = (
    (ABOVE, MINE, 0),
    (ACROSS, MINE, 0),
    (None, PARTNER, 0),
    (ACROSS, PARTNER, 0),
    (ABOVE, MINE, 1),
    (None, PARTNER, 1),
    (NOISY, MINE, 0),
    (ACROSS, PARTNER, 1),
    (ACROSS, MINE, 1),
    (NOISY, MINE, 1),
    (NOISY, MINE, 2),
    (None, PARTNER, 2),
    (ACROSS, PARTNER, 2),
)
PASS_ON = {0: (2, 3), 1: (4,), 3: (5,), 4: (6, 7), 5: (8,), 6: (9,), 8: (10,), 11: (11,)}
HAND_OVER_AFTER = {3: 0, 7: 1}
MERGE_AFTER = {9: 0}


def lookup(step, values):
    out = jnp.int32(values[0])
    for i, value in enumerate(values):
        if i and value != values[0]:
            out = jnp.where(step == i, jnp.int32(value), out)
    return out


def validity(group, lengths_ref, pattern_ref):
    videos = lengths_ref.shape[0]
    video, end = jnp.int32(0), jnp.int32(0)
    starts = []
    for j in range(videos):
        starts.append(end)
        end = end + lengths_ref[j]
        video = video + jnp.where(end <= group, 1, 0)
    first = jnp.int32(0)
    row = [jnp.int32(0)] * REACH
    for j in range(videos):
        first = jnp.where(video == j, starts[j], first)
        row = [jnp.where(video == j, pattern_ref[j, h], row[h]) for h in range(REACH)]
    return [(group - (h + 1) >= first) & (row[h] == 1) for h in range(REACH)]


def kernel(
    groups, heads_axis,
    noisy_ref, clean_ref, lengths_ref, pattern_ref, out_ref,
    paired, query, keyval, accum, peak, total, part, part_stat, got, got_stat, final, even_scores, odd_scores, weights,
    noisy_send, noisy_recv, clean_send, clean_recv, query_send, query_recv,
    part_send, part_recv, out_send, out_recv, local_sem,
):
    group, head = lax.axis_index("group"), lax.axis_index("head")
    rows = noisy_ref.shape[1]
    tokens, width = query.shape[1:]
    heads_here = width // HEAD_DIM
    column = lax.rem(group, ROW)
    odd = lax.rem(column, 2)
    near = group + 1 - 2 * odd
    far = group - column + (ROW - 1) - column
    below = lax.rem(group + ROW, groups)
    above = lax.rem(group + groups - ROW, groups)
    first_row, sends_below = group < ROW, group < groups - ROW
    peers = [lax.rem(head + k, heads_axis) for k in range(1, heads_axis)]

    mine_ok = validity(group, lengths_ref, pattern_ref)
    near_ok = validity(near, lengths_ref, pattern_ref)

    def remote(src, dst, send, recv, to_group, to_head):
        return pltpu.make_async_remote_copy(
            src_ref=src, dst_ref=dst, send_sem=send, recv_sem=recv,
            device_id=(to_group, to_head), device_id_type=MESH,
        )

    def columns(index):
        return pl.ds(pl.multiple_of(index * width, width), width)

    def lanes(h):
        return pl.ds(h * HEAD_DIM, HEAD_DIM)

    my_rows = pl.ds(pl.multiple_of(head * rows, rows), rows)

    def noisy_target(which):
        return query.at[MINE] if which == 0 else keyval.at[NOISY, which - 1]

    def noisy_copy(which, k):
        to = peers[k]
        return remote(
            noisy_ref.at[which, :, columns(to)], noisy_target(which).at[my_rows, :],
            noisy_send.at[which, k], noisy_recv.at[which, k], group, to,
        )

    def noisy_local(which):
        return pltpu.make_async_copy(
            noisy_ref.at[which, :, columns(head)], noisy_target(which).at[my_rows, :], local_sem.at[which]
        )

    def paired_copy(h):
        return pltpu.make_async_copy(clean_ref.at[:, h], paired.at[h], local_sem.at[3 + h])

    def part_pairs(h):
        n = 2 * HEAD_DIM
        rows_of = paired.at[h].reshape(2 * tokens, HEAD_DIM)
        to, source = (lax.broadcasted_iota(jnp.int32, (n, n), axis) for axis in (0, 1))
        pick = source == 2 * lax.rem(to, HEAD_DIM) + to // HEAD_DIM
        pick = jnp.where(pick, 1.0, 0.0).astype(keyval.dtype)
        for i in range(2 * tokens // n):
            moved = jnp.dot(pick, rows_of[pl.ds(i * n, n), :], preferred_element_type=jnp.float32)
            moved = moved.astype(keyval.dtype)
            for which in range(2):
                keyval[OWN, which, pl.ds(i * HEAD_DIM, HEAD_DIM), lanes(h)] = moved[which * HEAD_DIM:(which + 1) * HEAD_DIM]

    def piece(i):
        h, rest = divmod(i, 2 * SPLIT)
        which, part_of = divmod(rest, SPLIT)
        n = keyval.shape[2] // SPLIT
        return which, pl.ds(part_of * n, n), lanes(h)

    pieces = range(heads_here * 2 * SPLIT)

    def above_copy(i):
        at = piece(i)
        return remote(
            keyval.at[(OWN, *at)], keyval.at[(ABOVE, *at)], clean_send.at[0, i], clean_recv.at[0, i], below, head
        )

    def fill_copy(i):
        at = piece(i)
        return pltpu.make_async_copy(keyval.at[(OWN, *at)], keyval.at[(ABOVE, *at)], clean_recv.at[0, i])

    def across_copy(i, relay):
        at = piece(i)
        src = keyval.at[(ABOVE if relay else OWN, *at)]
        return remote(src, keyval.at[(ACROSS, *at)], clean_send.at[1, i], clean_recv.at[1, i], far, head)

    def query_copy(h):
        return remote(
            query.at[MINE, :, lanes(h)], query.at[PARTNER, :, lanes(h)],
            query_send.at[h], query_recv.at[h], near, head,
        )

    def part_copies(h, tile=None):
        at = pl.ds(0, tokens) if tile is None else pl.ds(tile * (tokens // TILES), tokens // TILES)
        sem = h if tile is None else h + tile
        return (
            remote(part.at[h, :, at], got.at[h, :, at], part_send.at[sem, 0], part_recv.at[sem, 0], near, head),
            remote(
                part_stat.at[h, :, at], got_stat.at[h, :, at], part_send.at[sem, 1], part_recv.at[sem, 1], near, head
            ),
        )

    def out_columns(h):
        return pl.ds(pl.multiple_of((head * heads_here + h) * HEAD_DIM, HEAD_DIM), HEAD_DIM)

    def out_copy(h, to):
        k = lax.rem(to - head + heads_axis, heads_axis)
        return remote(
            final.at[h, pl.ds(pl.multiple_of(to * rows, rows), rows), :], out_ref.at[:, out_columns(h)],
            out_send.at[h, k], out_recv.at[h, k], group, to,
        )

    def out_local(h):
        return pltpu.make_async_copy(final.at[h, my_rows, :], out_ref.at[:, out_columns(h)], local_sem.at[3 + heads_here + h])

    barrier = pltpu.get_barrier_semaphore()
    for to in peers:
        pl.semaphore_signal(barrier, inc=1, device_id=(group, to), device_id_type=MESH)
    for to in (near, far):
        pl.semaphore_signal(barrier, inc=1, device_id=(to, head), device_id_type=MESH)

    @pl.when(sends_below)
    def _():
        pl.semaphore_signal(barrier, inc=1, device_id=(below, head), device_id_type=MESH)

    @pl.when(~first_row)
    def _():
        pl.semaphore_signal(barrier, inc=1, device_id=(above, head), device_id_type=MESH)

    for h in range(heads_here):
        paired_copy(h).start()
    for which in range(3):
        noisy_local(which).start()
    others = range(len(peers))
    for h in range(heads_here):
        paired_copy(h).wait()
        part_pairs(h)
        if h == 0:
            pl.semaphore_wait(barrier, len(peers) + 2 + jnp.where(sends_below, 1, 0) + jnp.where(first_row, 0, 1))
        of_head = [i for i in pieces if i // (2 * SPLIT) == h]

        @pl.when(sends_below)
        def _():
            for i in of_head:
                above_copy(i).start()

        @pl.when(first_row)
        def _():
            for i in of_head:
                fill_copy(i).start()

        @pl.when(column < 2)
        def _():
            for i in of_head:
                across_copy(i, False).start()

        if h == 0:
            for k in others:
                noisy_copy(0, k).start()

    accum[...] = jnp.zeros_like(accum)
    total[...] = jnp.zeros_like(total)
    peak[...] = jnp.full_like(peak, -FAR)

    def pass_on(i):
        above_copy(i).wait_recv()

        @pl.when(column >= 2)
        def _():
            across_copy(i, True).start()

    for i in range(PASS_ON[0][0]):
        pass_on(i)
    noisy_local(0).wait()
    for k in others:
        noisy_copy(0, k).wait_recv()
    for h in range(heads_here):
        query_copy(h).start()
    for which in (1, 2):
        for k in others:
            noisy_copy(which, k).start()

    def lane_of(h):
        return pl.ds(pl.multiple_of(h * HEAD_DIM, HEAD_DIM), HEAD_DIM)

    def score(slot, whose, h, at):
        return lax.dot_general(
            keyval[slot, 0, :, lane_of(h)], query[whose, at, lane_of(h)], (((1,), (1,)), ((), ())),
            preferred_element_type=jnp.float32,
        )

    def weigh(slot, whose, h, keep, at, scores, largest):
        before = peak[whose, h, :, at]
        now = jnp.maximum(before, jnp.where(keep, largest, -FAR))
        expo = jnp.exp2((scores - jnp.where(keep, now, FAR)) * EXP2_SCALE)
        factor = jnp.exp2((before - now) * EXP2_SCALE)
        added = lax.dot_general(
            keyval[slot, 1, :, lane_of(h)], expo.astype(jnp.bfloat16), (((0,), (0,)), ((), ())),
            preferred_element_type=jnp.float32,
        )
        peak[whose, h, :, at] = now
        total[whose, h, :, at] = total[whose, h, :, at] * factor + jnp.sum(expo, axis=0, keepdims=True)
        accum[whose, h, :, at] = accum[whose, h, :, at] * factor + added

    def attend(slot, whose, h, keep, at):
        scores = score(slot, whose, h, at)
        weigh(slot, whose, h, keep, at, scores, jnp.max(scores, axis=0, keepdims=True))

    every = pl.ds(0, tokens)

    def tile_of(t):
        return pl.ds(t * (tokens // TILES), tokens // TILES)

    def merge(h, tile=None):
        at = every if tile is None else tile_of(tile)
        for copy in part_copies(h, tile):
            copy.wait_recv()
        here, there = peak[MINE, h, :, at], got_stat[h, 0:1, at]
        now = jnp.maximum(here, there)
        a = jnp.exp2((here - now) * EXP2_SCALE)
        b = jnp.exp2((there - now) * EXP2_SCALE)
        inverse = 1.0 / (total[MINE, h, :, at] * a + got_stat[h, 1:2, at] * b)
        summed = accum[MINE, h, :, at] * (a * inverse) + got[h, :, at].astype(jnp.float32) * (b * inverse)
        final[h, at, :] = jnp.transpose(summed).astype(final.dtype)
        for j in range(at.start // rows, (at.start + at.size) // rows):

            @pl.when(head != j)
            def _():
                out_copy(h, j).start()

            @pl.when(head == j)
            def _():
                out_local(h).start()

    def hand_over(h, tile=None):
        at = every if tile is None else tile_of(tile)
        part[h, :, at] = accum[PARTNER, h, :, at].astype(part.dtype)
        part_stat[h, 0:1, at] = peak[PARTNER, h, :, at]
        part_stat[h, 1:2, at] = total[PARTNER, h, :, at]
        for copy in part_copies(h, tile):
            copy.start()

    def take_across(h, which=None):
        for i in pieces:
            if i // (2 * SPLIT) == h and which in (None, i // SPLIT % 2):
                across_copy(i, False).wait_recv()

    def take_noisy():
        for which in (1, 2):
            noisy_local(which).wait()
            for k in others:
                noisy_copy(which, k).wait_recv()

    hooks = {}
    seen = set()
    for i, (slot, whose, h) in enumerate(STEPS[:-1]):
        todo = hooks.setdefault(i, [])
        for j in PASS_ON.get(i, ()):
            todo.append(functools.partial(pass_on, j))
        if whose == PARTNER and ("query", h) not in seen:
            seen.add(("query", h))
            todo.append(functools.partial(lambda h: query_copy(h).wait_recv(), h))
        if slot == ACROSS and ("across", h) not in seen:
            seen.add(("across", h))
            todo.append(functools.partial(take_across, h))
        if slot == NOISY and "noisy" not in seen:
            seen.add("noisy")
            todo.append(take_noisy)
    after = {}
    for i, h in HAND_OVER_AFTER.items():
        after.setdefault(i, []).append(functools.partial(hand_over, h))
    for i, h in MERGE_AFTER.items():
        after.setdefault(i, []).append(functools.partial(merge, h))

    def distance(slot, whose, is_odd):
        if slot == NOISY:
            return -1
        if whose == MINE:
            return 3 if slot == ABOVE else (2 if is_odd else 0)
        return 1 if slot == ACROSS else (2 if is_odd else 0)

    def run(actions, step, parity):
        for i, todo in actions.items():
            if todo and i % 2 == parity:

                @pl.when(step == i)
                def _():
                    for act in todo:
                        act()

    def operands(step):
        shared = jnp.where(odd == 1, ABOVE, OWN)
        slot = lookup(step, [-1 if s is None else s for s, _, _ in STEPS])
        slot = jnp.where(slot < 0, shared, slot)
        return slot, lookup(step, [w for _, w, _ in STEPS]), lookup(step, [h for _, _, h in STEPS])

    def kept(step, whose):
        at = jnp.where(
            odd == 1,
            lookup(step, [distance(s, w, True) for s, w, _ in STEPS]),
            lookup(step, [distance(s, w, False) for s, w, _ in STEPS]),
        )
        keep = at < 0
        for j in range(REACH):
            keep = keep | ((at == j) & jnp.where(whose == MINE, mine_ok[j], near_ok[j]))
        return keep

    def begin(step, held):
        return begin_at(*operands(step), held)

    def begin_at(slot, whose, h, held):
        scores = score(slot, whose, h, every)
        held[...] = scores
        return jnp.max(scores, axis=0, keepdims=True)

    def finish(step, held, largest):
        slot, whose, h = operands(step)
        weigh(slot, whose, h, kept(step, whose), every, held[...], largest)

    def two(pair, largest):
        step = 2 * pair
        run(hooks, step + 1, 1)
        following = begin(step + 1, odd_scores)
        finish(step, even_scores, largest)
        run(after, step, 0)
        run(hooks, step + 2, 0)
        largest = begin(step + 2, even_scores)
        finish(step + 1, odd_scores, following)
        run(after, step + 1, 1)
        return largest

    for act in hooks.pop(0):
        act()
    largest = begin(0, even_scores)
    final_steps = len(STEPS) - 2
    largest = lax.fori_loop(0, final_steps // 2, two, largest)

    last = heads_here - 1
    for act in hooks.pop(final_steps):
        act()
    following = begin(final_steps, odd_scores)
    finish(final_steps - 1, even_scores, largest)
    take_across(last, 0)
    largest = begin(final_steps + 1, even_scores)
    finish(final_steps, odd_scores, following)

    before = peak[PARTNER, last]
    now = jnp.maximum(before, jnp.where(near_ok[1], largest, -FAR))
    expo = jnp.exp2((even_scores[...] - jnp.where(near_ok[1], now, FAR)) * EXP2_SCALE)
    factor = jnp.exp2((before - now) * EXP2_SCALE)
    weights[...] = expo.astype(weights.dtype)
    peak[PARTNER, last] = now
    total[PARTNER, last] = total[PARTNER, last] * factor + jnp.sum(expo, axis=0, keepdims=True)
    following = begin_at(ABOVE, MINE, last, odd_scores)
    largest = begin_at(ACROSS, MINE, last, even_scores)
    take_across(last, 1)
    for tile in range(TILES):
        at = tile_of(tile)
        added = lax.dot_general(
            keyval[ACROSS, 1, :, lanes(last)], weights[:, at], (((0,), (0,)), ((), ())),
            preferred_element_type=jnp.float32,
        )
        n = tokens // TILES
        accum[PARTNER, last, :, at] = accum[PARTNER, last, :, at] * factor[:, tile * n:(tile + 1) * n] + added
        hand_over(last, tile)
    weigh(ABOVE, MINE, last, mine_ok[3], every, odd_scores[...], following)
    merge(1)
    keep = (mine_ok[0] & (odd == 0)) | (mine_ok[2] & (odd == 1))
    weigh(ACROSS, MINE, last, keep, every, even_scores[...], largest)
    for tile in range(TILES):
        merge(last, tile)

    for h in range(heads_here):
        out_local(h).wait()
        query_copy(h).wait_send()
        for copy in [c for t in range(TILES) for c in part_copies(h, t)] if h == last else part_copies(h):
            copy.wait_send()
        for k in others:
            out_copy(h, peers[k]).wait()
            noisy_copy(h, k).wait_send()
    for i in pieces:
        across_copy(i, False).wait_send()

    @pl.when(sends_below)
    def _():
        for i in pieces:
            above_copy(i).wait_send()


def on_device(groups, heads_axis, noisy_qkv, clean_kv, video_lengths, pattern):
    noisy = jnp.transpose(noisy_qkv, (1, 0, 2))
    tokens, _, width = clean_kv.shape
    heads_here = width // HEAD_DIM
    clean = jnp.transpose(clean_kv.reshape(tokens, 2, heads_here, HEAD_DIM), (0, 2, 1, 3))
    rows, features = noisy.shape[1:]
    dma = pltpu.SemaphoreType.DMA
    peers = heads_axis - 1
    flops = 2 * 2 * tokens * tokens * width * (REACH + 1)
    return pl.pallas_call(
        functools.partial(kernel, groups, heads_axis),
        out_shape=jax.ShapeDtypeStruct((rows, features), noisy.dtype),
        in_specs=[pl.BlockSpec(memory_space=pl.ANY)] * 2 + [pl.BlockSpec(memory_space=pltpu.SMEM)] * 2,
        out_specs=pl.BlockSpec(memory_space=pl.ANY),
        scratch_shapes=[
            pltpu.VMEM((heads_here, tokens, 2, HEAD_DIM), noisy.dtype),
            pltpu.VMEM((2, tokens, width), noisy.dtype),
            pltpu.VMEM((4, 2, tokens, width), noisy.dtype),
            pltpu.VMEM((2, heads_here, HEAD_DIM, tokens), jnp.float32),
            pltpu.VMEM((2, heads_here, 1, tokens), jnp.float32),
            pltpu.VMEM((2, heads_here, 1, tokens), jnp.float32),
            pltpu.VMEM((heads_here, HEAD_DIM, tokens), noisy.dtype),
            pltpu.VMEM((heads_here, 2, tokens), jnp.float32),
            pltpu.VMEM((heads_here, HEAD_DIM, tokens), noisy.dtype),
            pltpu.VMEM((heads_here, 2, tokens), jnp.float32),
            pltpu.VMEM((heads_here, tokens, HEAD_DIM), noisy.dtype),
            pltpu.VMEM((tokens, tokens), jnp.float32),
            pltpu.VMEM((tokens, tokens), jnp.float32),
            pltpu.VMEM((tokens, tokens), noisy.dtype),
            dma((3, peers)), dma((3, peers)),
            dma((2, heads_here * 2 * SPLIT)), dma((2, heads_here * 2 * SPLIT)),
            dma((heads_here,)), dma((heads_here,)),
            dma((heads_here - 1 + TILES, 2)), dma((heads_here - 1 + TILES, 2)),
            dma((heads_here, heads_axis)), dma((heads_here, heads_axis)),
            dma((3 + 2 * heads_here,)),
        ],
        compiler_params=pltpu.CompilerParams(
            collective_id=0, has_side_effects=True, vmem_limit_bytes=56 * 2**20
        ),
        cost_estimate=pl.CostEstimate(
            flops=flops, bytes_accessed=8 * tokens * width, transcendentals=tokens * tokens * heads_here * (REACH + 1)
        ),
    )(noisy, clean, video_lengths, pattern)


def solution(mesh):
    groups, heads_axis = mesh.shape["group"], mesh.shape["head"]
    return jax.shard_map(
        functools.partial(on_device, groups, heads_axis),
        mesh=mesh,
        in_specs=(P(("group", "head"), None, None), P("group", None, "head"), P(), P()),
        out_specs=P(("group", "head"), None),
        check_vma=False,
    )
```
